128 devices in a mesh: dp: 16 (over y, z), tp: 8 (over x, core).
Axes of the slice: x: 4, y: 4, z: 4, core: 2. Of those that a mesh axis runs over, the one named last changes fastest.
Arguments:
- residual_in: bfloat16 [1024, 7168], P(('dp', 'tp')), may hold values from -6 to 6
- query_latent: bfloat16 [1024, 64, 576], P(('dp', 'tp')), may hold values from -48 to 48
- latent_cache: bfloat16 [1024, 384, 576], P(('dp', 'tp')), may hold values from -6 to 6
- new_latent: bfloat16 [1024, 576], P(('dp', 'tp')), may hold values from -6 to 6
- context_lengths: int32 [1024], P(('dp', 'tp')), may hold values from 1 to 384, 196608 in all
- value_up: bfloat16 [64, 512, 128], P('tp'), may hold values from -0.25 to 0.25
- out_proj: bfloat16 [8192, 7168], P('tp'), may hold values from -0.0625 to 0.0625
- norm_gain: bfloat16 [7168], replicated, may hold values from 0.099609375 to 1.8984375
- expert_ids: int32 [1024, 8], P(('dp', 'tp')), may hold values from 0 to 15, all different within a row
- route_scores: float32 [1024, 8], P(('dp', 'tp')), may hold values from 0.2 to 1
- expert_slots: int32 [16], replicated, may hold values from 0 to 15, each once
- expert_gate_up: bfloat16 [16, 2, 7168, 1024], P('dp', None, None, 'tp'), may hold values from -0.0625 to 0.0625
- expert_down: bfloat16 [16, 1024, 7168], P('dp', 'tp'), may hold values from -0.1875 to 0.1875
Outputs:
- attention_out: bfloat16 [1024, 7168], P(('dp', 'tp'))
- layer_output: bfloat16 [1024, 7168], P(('dp', 'tp'))
The draws below stay inside these ranges and needn't reach their ends.
All inputs are finite; a program needn't handle non-finite values. No bound on the sum of `context_lengths` on one device may be relied on, other than what follows from the above.
Results may differ from the reference program's by a relative error of at most 0.02.
Values may be sent and summed in bfloat16 or wider, within the bound.
No kernel may reach another device: no remote copies, remote signals or barrier semaphores. Data moves between devices by JAX's collectives and lax.ppermute only.
A program may use at most 128 MiB of HBM per device.

```python
import math
import jax
import jax.numpy as jnp
import numpy as np
from jax import lax

D = 7168
HEADS = 64
LATENT = 512
ROPE = 64
VHEAD = 128
EXPERT_FF = 1024
TOP = 8
CTX = 384
EXPERTS = 16
TOKENS = 1024
N_TP = 8


def draw_latent_cache(key, part):
    own_key = jax.random.fold_in(key, 1)
    key_width = LATENT + ROPE
    cache_vals = jnp.clip(jax.random.normal(own_key, (TOKENS, CTX, key_width), jnp.float32), -6.0, 6.0)
    return cache_vals.astype(jnp.bfloat16)


def draw_new_latent(key, part):
    own_key = jax.random.fold_in(key, 2)
    key_width = LATENT + ROPE
    fresh_vals = jnp.clip(jax.random.normal(own_key, (TOKENS, key_width), jnp.float32), -6.0, 6.0)
    return fresh_vals.astype(jnp.bfloat16)


def draw_query_latent(key, part):
    own_key = jax.random.fold_in(key, 3)
    key_width = LATENT + ROPE
    query_vals = jnp.clip(jax.random.normal(own_key, (TOKENS, HEADS, key_width), jnp.float32), -6.0, 6.0)
    return query_vals.astype(jnp.bfloat16)


def steps_of(key, dims, split, low, top_value):
    loudness, own = 1.0, jax.random.fold_in(key, 6)
    for axis_at, shards_of in split:
        steps = jnp.exp(jax.random.uniform(jax.random.fold_in(own, axis_at), (shards_of,), jnp.float32, low / len(split), top_value / len(split)))
        loudness = loudness * jnp.repeat(steps, dims[axis_at] // shards_of).reshape([-1 if axis == axis_at else 1 for axis in range(len(dims))])
    return loudness


def picks_of(rng, rows, amount, top, lift):
    sequence = jax.random.permutation(jax.random.fold_in(rng, 1), amount)
    boost = sequence
    for power in range(3):
        boost = boost * boost // amount
    boost = boost * lift // amount
    tickets = jax.random.randint(jax.random.fold_in(rng, 2), (rows, amount), 0, 4096) + boost
    fixed_rows = jax.random.permutation(jax.random.fold_in(rng, 3), rows)[jnp.arange(amount) % rows]
    tickets = jnp.where(jnp.arange(rows)[:, None] == fixed_rows[None, :], 1 << 14, tickets)
    priority = tickets * amount + jnp.arange(amount)
    return lax.top_k(priority.astype(jnp.int32), top)[1].astype(jnp.int32)


def split_up(count, total, most, skew):
    loads = [(1 << 20) // math.isqrt(grade ** skew) + 1 for grade in range(2, count + 1)]
    surplus, counts = total - most - (count - 1), [1] * (count - 1)
    while surplus > 0:
        free = [i for i in range(count - 1) if counts[i] < most]
        pool, budget = sum([loads[i] for i in free]), surplus
        for i in free:
            addition = min(most - counts[i], max(1, budget * loads[i] // pool), surplus)
            counts[i] = counts[i] + addition
            surplus = surplus - addition
    return np.array([most] + counts)


def ragged(rng, number_of, total, most, skew):
    if number_of == 2:
        one = jax.random.randint(rng, (), max(1, total - most), min(most, total - 1) + 1)
        return jnp.stack([one, total - one])
    sizes = jnp.asarray(split_up(number_of, total, most, skew), jnp.int32)
    twos = (number_of - 1) // 2
    donor, receiver = sizes[1:1 + 2 * twos:2], sizes[2:2 + 2 * twos:2]
    room = jnp.minimum(donor - 1, most - receiver)
    passed = jax.random.randint(jax.random.fold_in(rng, 1), (twos,), 0, 1 << 20) % (room + 1)
    sizes = sizes.at[1:1 + 2 * twos:2].set(donor - passed).at[2:2 + 2 * twos:2].set(receiver + passed)
    return sizes[jax.random.permutation(jax.random.fold_in(rng, 2), number_of)]


def normal_values(rng, extent, scale, reach, cuts=(), held_as=jnp.bfloat16):
    gain = steps_of(rng, extent, cuts, -0.22, 0.18) if cuts else 1.0
    drawn = jax.random.normal(rng, extent, jnp.float32) * scale * gain
    return jnp.minimum(jnp.maximum(drawn, -reach), reach).astype(held_as)


def setup_inputs(seed: int = 0) -> dict:
    key_of = jax.random.split(jax.random.key(seed), 14)
    return {
        "residual_in": normal_values(key_of[0], (TOKENS, D), 1.0, 6.0, ((0, 128),)),
        "query_latent": draw_query_latent(jax.random.fold_in(key_of[13], 71), 0),
        "latent_cache": draw_latent_cache(jax.random.fold_in(key_of[13], 71), 0),
        "new_latent": draw_new_latent(jax.random.fold_in(key_of[13], 71), 0),
        "context_lengths": ragged(key_of[4], TOKENS, TOKENS * CTX // 2, CTX, 2).astype(jnp.int32),
        "value_up": normal_values(key_of[5], (HEADS, LATENT, VHEAD), LATENT ** -0.5, 0.25, ((0, 8),)),
        "out_proj": normal_values(key_of[6], (HEADS * VHEAD, D), (HEADS * VHEAD) ** -0.5, 0.0625, ((0, 8),)),
        "norm_gain": jnp.clip(1.0 + 0.18 * jax.random.normal(key_of[7], (D,), jnp.float32), 0.099609375, 1.8984375).astype(jnp.bfloat16),
        "expert_ids": picks_of(key_of[8], TOKENS, EXPERTS, TOP, 8192),
        "route_scores": jnp.clip(jnp.exp(math.log(1.0) - 1.609438 * jax.random.uniform(key_of[9], (TOKENS, TOP), jnp.float32) ** steps_of(key_of[9], (TOKENS, TOP), ((0, 128),), -0.2, 0.2)), 0.2, 1.0),
        "expert_slots": jax.random.permutation(key_of[10], EXPERTS).astype(jnp.int32),
        "expert_gate_up": normal_values(key_of[11], (EXPERTS, 2, D, EXPERT_FF), D ** -0.5, 0.0625, ((0, 16), (3, 8))),
        "expert_down": normal_values(key_of[12], (EXPERTS, EXPERT_FF, D), EXPERT_FF ** -0.5, 0.1875, ((0, 16), (1, 8))),
    }


score_scale = 192.0 ** (-0.5)
route_scale = 2.5
norm_eps = 1e-06

def attend_one(pieces):
    query_rows, cache_rows, fresh_key, length = pieces
    query_rows = query_rows.astype(jnp.float32)
    cache_rows = cache_rows.astype(jnp.float32)
    fresh_key = fresh_key.astype(jnp.float32)
    scores = jnp.dot(query_rows, cache_rows.T, precision=lax.Precision.HIGHEST) * score_scale
    own_score = jnp.dot(query_rows, fresh_key, precision=lax.Precision.HIGHEST) * score_scale
    positions = lax.broadcasted_iota(jnp.int32, scores.shape, 1)
    scores = jnp.where(positions < length, scores, -jnp.inf)
    row_max = jnp.maximum(lax.optimization_barrier(jnp.max(scores, axis=1)), own_score)
    cache_weights = jnp.exp(scores - row_max[:, None])
    own_weight = jnp.exp(own_score - row_max)
    denominator = lax.optimization_barrier(jnp.sum(cache_weights, axis=1)) + own_weight
    cache_weights = (cache_weights / denominator[:, None]).astype(jnp.bfloat16)
    own_weight = (own_weight / denominator).astype(jnp.bfloat16)
    cache_weights = lax.optimization_barrier(cache_weights).astype(jnp.float32)
    own_weight = lax.optimization_barrier(own_weight).astype(jnp.float32)
    result = jnp.dot(cache_weights, cache_rows[:, :LATENT], precision=lax.Precision.HIGHEST)
    result = result + own_weight[:, None] * fresh_key[None, :LATENT]
    return result.astype(jnp.bfloat16)

def combine_table(expert_ids, gates, expert_slots):
    slot_count = expert_slots.shape[0]
    labels = lax.broadcasted_iota(jnp.int32, (1, 1, slot_count), 2)
    slot_of = lax.optimization_barrier(jnp.sum(jnp.where(expert_ids[:, :, None] == labels, expert_slots[None, None, :], 0), axis=2))
    slot_hits = slot_of[:, :, None] == labels
    weight_table = lax.optimization_barrier(jnp.sum(jnp.where(slot_hits, gates[:, :, None].astype(jnp.float32), 0.0), axis=1))
    return weight_table.astype(jnp.bfloat16)

def reference(residual_in, query_latent, latent_cache, new_latent, context_lengths, value_up, out_proj, norm_gain, expert_ids, route_scores, expert_slots, expert_gate_up, expert_down):
    latent_out = lax.map(attend_one, (query_latent, latent_cache, new_latent, context_lengths))
    values = jnp.einsum('thl,hlv->thv', latent_out.astype(jnp.float32), value_up.astype(jnp.float32), precision=lax.Precision.HIGHEST).astype(jnp.bfloat16)
    values = values.reshape(TOKENS, HEADS * VHEAD)
    attention_out = jnp.dot(values, out_proj, preferred_element_type=jnp.float32).astype(jnp.bfloat16)
    residual_mid = (residual_in.astype(jnp.float32) + attention_out.astype(jnp.float32)).astype(jnp.bfloat16)
    residual_f32 = residual_mid.astype(jnp.float32)
    scaling = lax.rsqrt(lax.optimization_barrier(jnp.mean(residual_f32 * residual_f32, axis=1, keepdims=True)) + norm_eps)
    normed = (residual_f32 * scaling * norm_gain.astype(jnp.float32)[None, :]).astype(jnp.bfloat16)
    gates = (route_scale * route_scores / lax.optimization_barrier(jnp.sum(route_scores, axis=1, keepdims=True))).astype(jnp.bfloat16)
    weight_table = combine_table(expert_ids, gates, expert_slots)

    def expert_step(running, pieces):
        gate_up, down_rows, column = pieces
        gate_part = jnp.dot(normed, gate_up[0], preferred_element_type=jnp.float32)
        up_part = jnp.dot(normed, gate_up[1], preferred_element_type=jnp.float32)
        activated = (jax.nn.silu(gate_part) * up_part).astype(jnp.bfloat16)
        activated = activated.reshape(TOKENS, N_TP, EXPERT_FF // N_TP).astype(jnp.float32)
        slices = down_rows.reshape(N_TP, EXPERT_FF // N_TP, D).astype(jnp.float32)
        partial_value = jnp.einsum('tjf,jfd->tjd', activated, slices, precision=lax.Precision.HIGHEST).astype(jnp.bfloat16)
        summed = lax.optimization_barrier(jnp.sum(partial_value.astype(jnp.float32), axis=1))
        return (running + column.astype(jnp.float32)[:, None] * summed, None)
    start_sum = jnp.zeros((TOKENS, D), jnp.float32)
    expert_sum, _ = lax.scan(expert_step, start_sum, (expert_gate_up, expert_down, weight_table.T))
    layer_output = (residual_mid.astype(jnp.float32) + expert_sum).astype(jnp.bfloat16)
    return (attention_out, layer_output)
```

```python
import jax
import jax.numpy as jnp
from jax import lax
from jax.sharding import Mesh, PartitionSpec as P

score_scale = 192.0 ** (-0.5)
route_scale = 2.5
norm_eps = 1e-06
f32 = jnp.float32
bf16 = jnp.bfloat16


def attend(query_rows, cache_rows, fresh_key, context_lengths, latent_width):
    scores = (
        jnp.einsum("rhc,rtc->rht", query_rows, cache_rows, preferred_element_type=jnp.float32)
        * score_scale
    )
    own_score = (
        jnp.einsum("rhc,rc->rh", query_rows, fresh_key, preferred_element_type=jnp.float32)
        * score_scale
    )
    positions = lax.broadcasted_iota(jnp.int32, scores.shape, 2)
    scores = jnp.where(positions < context_lengths[:, None, None], scores, -jnp.inf)
    row_max = jnp.maximum(jnp.max(scores, axis=2), own_score)
    cache_weights = jnp.exp(scores - row_max[:, :, None])
    own_weight = jnp.exp(own_score - row_max)
    denominator = jnp.sum(cache_weights, axis=2) + own_weight
    cache_weights = (cache_weights / denominator[:, :, None]).astype(jnp.bfloat16)
    own_weight = (own_weight / denominator).astype(jnp.bfloat16)
    own_weight = lax.optimization_barrier(own_weight).astype(jnp.float32)
    result = jnp.einsum(
        "rht,rtl->rhl",
        cache_weights,
        cache_rows[:, :, :latent_width],
        preferred_element_type=jnp.float32,
    )
    result = result + own_weight[:, :, None] * fresh_key[:, None, :latent_width].astype(jnp.float32)
    return result.astype(jnp.bfloat16)


def combine_table(expert_ids, gates, expert_slots):
    slot_count = expert_slots.shape[0]
    labels = lax.broadcasted_iota(jnp.int32, (1, 1, slot_count), 2)
    slot_of = jnp.sum(
        jnp.where(expert_ids[:, :, None] == labels, expert_slots[None, None, :], 0), axis=2
    )
    slot_hits = slot_of[:, :, None] == labels
    weight_table = jnp.sum(jnp.where(slot_hits, gates[:, :, None].astype(jnp.float32), 0.0), axis=1)
    return weight_table.astype(jnp.bfloat16)


def shift(value, axis, distance):
    count = lax.axis_size(axis)
    return lax.ppermute(value, axis, [((i + distance) % count, i) for i in range(count)])


def swap(value):
    return lax.ppermute(value, "core", [(0, 1), (1, 0)])


def total(*terms):
    return sum(term.astype(f32) for term in terms)


def gather_near(block, axis):
    return jnp.concatenate(
        [block, shift(block, axis, 1), shift(block, axis, 2), shift(block, axis, -1)], axis=0
    )


def gather_far(block, axis):
    half = block.shape[0] // 2
    right, left = shift(block, axis, 1), shift(block, axis, -1)
    low, high = shift(right[:half], axis, 1), shift(left[half:], axis, -1)
    return [block, right, jnp.concatenate([low, high], axis=0), left]


def scatter_far(own, right, opposite, left, axis):
    half = own.shape[0] // 2
    low, high = shift(opposite[:half], axis, -1), shift(opposite[half:], axis, 1)
    right = jnp.concatenate([total(right[:half], low).astype(bf16), right[half:]], axis=0)
    left = jnp.concatenate([left[:half], total(left[half:], high).astype(bf16)], axis=0)
    return total(own, shift(right, axis, -1), shift(left, axis, 1)).astype(bf16)


def scatter_near(value, axis):
    return total(
        value[0], shift(value[1], axis, -1), shift(value[2], axis, 2), shift(value[3], axis, 1)
    ).astype(bf16)


def per_device(
    residual_in,
    query_latent,
    latent_cache,
    new_latent,
    context_lengths,
    value_up,
    out_proj,
    norm_gain,
    expert_ids,
    route_scores,
    expert_slots,
    expert_gate_up,
    expert_down,
):
    rows, model_width = residual_in.shape
    latent_width = value_up.shape[1]
    half = model_width // 2
    lanes = 128
    core = lax.axis_index("core")
    x_at = lax.axis_index("x")
    expert_at = lax.axis_index("y") * 4 + lax.axis_index("z")

    def mine(value, axis):
        return lax.dynamic_slice_in_dim(value, core * half, half, axis=axis)

    def others(value, axis):
        return lax.dynamic_slice_in_dim(value, (1 - core) * half, half, axis=axis)

    def whole(own, got):
        return jnp.where(
            core == 0,
            jnp.concatenate([own, got], axis=1),
            jnp.concatenate([got, own], axis=1),
        )

    gates = (route_scale * route_scores / jnp.sum(route_scores, axis=1, keepdims=True)).astype(bf16)
    table = combine_table(expert_ids, gates, expert_slots)
    slots = table.shape[1]

    latent_out = attend(query_latent, latent_cache, new_latent, context_lengths, latent_width)
    exchanged = lax.all_to_all(latent_out, ("x", "core"), split_axis=1, concat_axis=0, tiled=True)

    gate_up = expert_gate_up[0]
    down = expert_down[0]
    gate_up_own = mine(gate_up, 1)
    gate_up_got = swap(others(gate_up, 1))
    weight_in = jnp.concatenate(
        [gate_up_own[0], gate_up_own[1], gate_up_got[0], gate_up_got[1]], axis=1
    )
    weight_in = jnp.pad(weight_in, ((0, lanes), (0, 0)))
    weight_out = jnp.concatenate([mine(down, 1), swap(others(down, 1))], axis=0)

    residual_own, residual_got = mine(residual_in, 1), swap(others(residual_in, 1))
    residual_chip = jnp.where(
        core == 0,
        jnp.stack([residual_own, residual_got]),
        jnp.stack([residual_got, residual_own]),
    )
    group_table = lax.all_gather(table, ("x", "core"), axis=0, tiled=True)
    group_table = jnp.pad(group_table, ((0, 0), (0, lanes - slots))).reshape(4, 2, rows, lanes)

    values = jnp.einsum(
        "thl,hlv->thv", exchanged, value_up, preferred_element_type=f32
    ).astype(bf16)
    values = values.reshape(values.shape[0], values.shape[1] * values.shape[2])
    projected = jnp.dot(values, out_proj, preferred_element_type=f32)
    chip_sum = mine(projected, 1) + swap(others(projected, 1).astype(bf16)).astype(f32)
    chip_sum = chip_sum.reshape(4, 2, rows, half)
    own_place = (lax.broadcasted_iota(jnp.int32, (4, 1, 1), 0) == x_at)
    gain = mine(norm_gain, 0).astype(f32)

    attention_parts, gathered = [], []
    for part in range(2):
        part_sum = chip_sum[:, part]
        sent = (part_sum + jnp.where(own_place, residual_chip[part][None].astype(f32), 0.0)).astype(bf16)
        arrived = [shift(sent, "x", d) for d in (1, 2, -1)]
        own_rows = lambda v: lax.dynamic_index_in_dim(v, x_at, axis=0, keepdims=False)
        attention_parts.append(
            total(own_rows(part_sum), *[own_rows(v) for v in arrived]).astype(bf16)
        )
        residual_f32 = total(sent, *arrived).astype(bf16).astype(f32)
        squares = jnp.sum(residual_f32 * residual_f32, axis=2, keepdims=True)
        squares = squares + swap(squares)
        scaling = lax.rsqrt(squares / model_width + norm_eps)
        normed = (residual_f32 * scaling * gain[None, None, :]).astype(bf16)
        payload = jnp.concatenate([normed, group_table[:, part]], axis=2)
        gathered.append(payload.reshape(4 * rows, half + lanes))

    axes = (("y", "z"), ("z", "y"))
    near = [gather_near(gathered[p], axes[p][0]) for p in range(2)]
    far = [gather_far(near[p], axes[p][1]) for p in range(2)]

    back = []
    for part in range(2):
        blocks = far[part]
        products = [jnp.dot(b, weight_in, preferred_element_type=f32) for b in blocks]
        hidden = weight_in.shape[1] // 2
        got = swap(jnp.concatenate([p[:, hidden:].astype(bf16) for p in products], axis=0))
        product = jnp.concatenate([p[:, :hidden] for p in products], axis=0) + got.astype(f32)
        units = hidden // 2
        activated = (jax.nn.silu(product[:, :units]) * product[:, units:]).astype(bf16)
        activated = jnp.concatenate([activated, swap(activated)], axis=1)
        outs = []
        n = blocks[0].shape[0]
        for i, b in enumerate(blocks):
            weights = jnp.sum(
                jnp.where(
                    lax.broadcasted_iota(jnp.int32, (1, lanes), 1) == expert_at,
                    b[:, half:].astype(f32),
                    0.0,
                ),
                axis=1,
                keepdims=True,
            )
            out = jnp.dot(activated[i * n : (i + 1) * n], weight_out, preferred_element_type=f32)
            outs.append((out * weights).astype(bf16))
        back.append(outs)

    summed = [scatter_far(*back[p], axes[p][1]) for p in range(2)]
    summed = [scatter_near(summed[p].reshape(4, 4 * rows, half), axes[p][0]) for p in range(2)]
    to_x = jnp.stack([s.reshape(4, rows, half) for s in summed], axis=1)
    from_x = lax.all_to_all(to_x, "x", split_axis=0, concat_axis=0, tiled=True)
    chip_out = jnp.sum(from_x.astype(f32), axis=0)

    def to_tokens(own, other):
        return whole(own, swap(other))

    attention_out = to_tokens(
        jnp.where(core == 0, attention_parts[0], attention_parts[1]),
        jnp.where(core == 0, attention_parts[1], attention_parts[0]),
    )
    expert_sum = to_tokens(
        jnp.where(core == 0, chip_out[0], chip_out[1]).astype(bf16),
        jnp.where(core == 0, chip_out[1], chip_out[0]).astype(bf16),
    )
    residual_mid = total(residual_in, attention_out).astype(bf16)
    layer_output = total(residual_mid, expert_sum).astype(bf16)
    return (attention_out, layer_output)


def solution(mesh):
    torus = Mesh(mesh.devices.reshape(4, 4, 4, 2), ("y", "z", "x", "core"))
    dp, tp = ("y", "z"), ("x", "core")
    both = dp + tp
    placed = (
        P(both, None),
        P(both, None, None),
        P(both, None, None),
        P(both, None),
        P(both),
        P(tp, None, None),
        P(tp, None),
        P(),
        P(both, None),
        P(both, None),
        P(),
        P(dp, None, None, tp),
        P(dp, tp, None),
    )
    return jax.shard_map(
        per_device,
        mesh=torus,
        in_specs=placed,
        out_specs=(P(both, None), P(both, None)),
        check_vma=False,
    )
```

```python
import jax
import jax.numpy as jnp
from jax import lax
from jax.sharding import Mesh, PartitionSpec as P

score_scale = 192.0 ** (-0.5)
route_scale = 2.5
norm_eps = 1e-06
f32 = jnp.float32
bf16 = jnp.bfloat16


def attend(query_rows, cache_rows, fresh_key, context_lengths, latent_width):
    scores = (
        jnp.einsum("rhc,rtc->rht", query_rows, cache_rows, preferred_element_type=jnp.float32)
        * score_scale
    )
    own_score = (
        jnp.einsum("rhc,rc->rh", query_rows, fresh_key, preferred_element_type=jnp.float32)
        * score_scale
    )
    positions = lax.broadcasted_iota(jnp.int32, scores.shape, 2)
    scores = jnp.where(positions < context_lengths[:, None, None], scores, -jnp.inf)
    row_max = jnp.maximum(jnp.max(scores, axis=2), own_score)
    cache_weights = jnp.exp(scores - row_max[:, :, None])
    own_weight = jnp.exp(own_score - row_max)
    denominator = jnp.sum(cache_weights, axis=2) + own_weight
    cache_weights = (cache_weights / denominator[:, :, None]).astype(jnp.bfloat16)
    own_weight = (own_weight / denominator).astype(jnp.bfloat16)
    own_weight = lax.optimization_barrier(own_weight).astype(jnp.float32)
    result = jnp.einsum(
        "rht,rtl->rhl",
        cache_weights,
        cache_rows[:, :, :latent_width],
        preferred_element_type=jnp.float32,
    )
    result = result + own_weight[:, :, None] * fresh_key[:, None, :latent_width].astype(jnp.float32)
    return result.astype(jnp.bfloat16)


def combine_table(expert_ids, gates, expert_slots):
    slot_count = expert_slots.shape[0]
    labels = lax.broadcasted_iota(jnp.int32, (1, 1, slot_count), 2)
    slot_of = jnp.sum(
        jnp.where(expert_ids[:, :, None] == labels, expert_slots[None, None, :], 0), axis=2
    )
    slot_hits = slot_of[:, :, None] == labels
    weight_table = jnp.sum(jnp.where(slot_hits, gates[:, :, None].astype(jnp.float32), 0.0), axis=1)
    return weight_table.astype(jnp.bfloat16)


near_axis = ("y", "z")
far_axis = ("z", "y")


def ring(axes, distance):
    pairs = []
    for y in range(4):
        for z in range(4):
            for core in range(2):
                if axes[core] == "y":
                    source = ((y + distance) % 4, z)
                else:
                    source = (y, (z + distance) % 4)
                pairs.append(((source[0] * 4 + source[1]) * 2 + core, (y * 4 + z) * 2 + core))
    return pairs


def shift(value, axes, distance):
    if axes == "x":
        return lax.ppermute(value, "x", [((i + distance) % 4, i) for i in range(4)])
    return lax.ppermute(value, ("y", "z", "core"), ring(axes, distance))


def swap(value):
    return lax.ppermute(value, "core", [(0, 1), (1, 0)])


def total(*terms):
    return sum(term.astype(f32) for term in terms)


def gather_near(block, axes):
    return jnp.stack([block, shift(block, axes, 1), shift(block, axes, 2), shift(block, axes, -1)])


def gather_far(block, axes):
    half = block.shape[0] // 2
    right, left = shift(block, axes, 1), shift(block, axes, -1)
    low, high = shift(right[:half], axes, 1), shift(left[half:], axes, -1)
    return [block, right, jnp.concatenate([low, high], axis=0), left]


def scatter_far(own, right, opposite, left, axes):
    half = own.shape[0] // 2
    low, high = shift(opposite[:half], axes, -1), shift(opposite[half:], axes, 1)
    right = jnp.concatenate([total(right[:half], low).astype(bf16), right[half:]], axis=0)
    left = jnp.concatenate([left[:half], total(left[half:], high).astype(bf16)], axis=0)
    return total(own, shift(right, axes, -1), shift(left, axes, 1)).astype(bf16)


def scatter_near(value, axes):
    return total(
        value[0], shift(value[1], axes, -1), shift(value[2], axes, 2), shift(value[3], axes, 1)
    )


def per_device(
    residual_in,
    query_latent,
    latent_cache,
    new_latent,
    context_lengths,
    value_up,
    out_proj,
    norm_gain,
    expert_ids,
    route_scores,
    expert_slots,
    expert_gate_up,
    expert_down,
):
    rows, model_width = residual_in.shape
    latent_width = value_up.shape[1]
    half = model_width // 2
    lanes = 128
    core = lax.axis_index("core")
    x_at = lax.axis_index("x")
    expert_at = lax.axis_index("y") * 4 + lax.axis_index("z")

    def mine(value, axis):
        return lax.dynamic_slice_in_dim(value, core * half, half, axis=axis)

    def others(value, axis):
        return lax.dynamic_slice_in_dim(value, (1 - core) * half, half, axis=axis)

    def by_core(own, got):
        return jnp.where(core == 0, jnp.stack([own, got]), jnp.stack([got, own]))

    def to_tokens(chip):
        own = jnp.where(core == 0, chip[0], chip[1])
        got = swap(jnp.where(core == 0, chip[1], chip[0]))
        return jnp.where(
            core == 0,
            jnp.concatenate([own, got], axis=1),
            jnp.concatenate([got, own], axis=1),
        )

    gates = (route_scale * route_scores / jnp.sum(route_scores, axis=1, keepdims=True)).astype(bf16)
    table = combine_table(expert_ids, gates, expert_slots)
    table = jnp.pad(table, ((0, 0), (0, lanes - table.shape[1])))

    latent_out = attend(query_latent, latent_cache, new_latent, context_lengths, latent_width)
    exchanged = lax.all_to_all(latent_out, ("x", "core"), split_axis=1, concat_axis=0, tiled=True)

    gate_up = expert_gate_up[0]
    down = expert_down[0]
    gate_up_own = mine(gate_up, 1)
    gate_up_got = swap(others(gate_up, 1))
    weight_in = jnp.concatenate(
        [gate_up_own[0], gate_up_own[1], gate_up_got[0], gate_up_got[1]], axis=1
    )
    weight_in = jnp.pad(weight_in, ((0, lanes), (0, 0)))
    weight_out = jnp.concatenate([mine(down, 1), swap(others(down, 1))], axis=0)

    chip_rows = by_core(
        jnp.concatenate([mine(residual_in, 1), table], axis=1),
        swap(jnp.concatenate([others(residual_in, 1), table], axis=1)),
    ).reshape(2 * rows, half + lanes)
    chip_residual, chip_table = chip_rows[:, :half], chip_rows[:, half:]

    values = jnp.einsum(
        "thl,hlv->thv", exchanged, value_up, preferred_element_type=f32
    ).astype(bf16)
    values = values.reshape(values.shape[0], values.shape[1] * values.shape[2])
    projected = jnp.dot(values, out_proj, preferred_element_type=f32)
    chip_sum = mine(projected, 1) + swap(others(projected, 1).astype(bf16)).astype(f32)
    chip_sum = chip_sum.reshape(4, 2 * rows, half)

    def for_chip(distance):
        place = lax.rem(x_at + distance, 4)
        return lax.dynamic_index_in_dim(chip_sum, place, axis=0, keepdims=False)

    attention = total(
        for_chip(0),
        shift(for_chip(1).astype(bf16), "x", -1),
        shift(for_chip(2).astype(bf16), "x", 2),
        shift(for_chip(3).astype(bf16), "x", 1),
    ).astype(bf16)
    residual_f32 = total(chip_residual, attention).astype(bf16).astype(f32)
    squares = jnp.sum(residual_f32 * residual_f32, axis=1, keepdims=True)
    squares = squares + swap(squares)
    scaling = lax.rsqrt(squares / model_width + norm_eps)
    gain = mine(norm_gain, 0).astype(f32)
    normed = (residual_f32 * scaling * gain[None, :]).astype(bf16)
    payload = jnp.concatenate([normed, chip_table], axis=1)

    width = half + lanes
    group = gather_near(payload, "x").reshape(8 * rows, width)
    near = gather_near(group, near_axis).reshape(4, 4, 2, rows, width)

    chunks = [near[:, :, c].reshape(16 * rows, width) for c in range(2)]
    hidden = weight_in.shape[1] // 2
    units = hidden // 2

    def crossed(value):
        value = value.reshape(4, 4, 4 * rows, value.shape[1])
        return value.transpose(1, 0, 2, 3).reshape(64 * rows, value.shape[3])

    sums = []
    for chunk in chunks:
        blocks = gather_far(chunk, far_axis)
        products = [jnp.dot(b, weight_in, preferred_element_type=f32) for b in blocks]
        got = swap(jnp.concatenate([p[:, hidden:].astype(bf16) for p in products], axis=0))
        product = jnp.concatenate([p[:, :hidden] for p in products], axis=0)
        product = product + crossed(got).astype(f32)
        activated = (jax.nn.silu(product[:, :units]) * product[:, units:]).astype(bf16)
        activated = jnp.concatenate([activated, crossed(swap(activated))], axis=1)
        outs = []
        n = 16 * rows
        for i, b in enumerate(blocks):
            weights = jnp.sum(
                jnp.where(
                    lax.broadcasted_iota(jnp.int32, (1, lanes), 1) == expert_at,
                    b[:, half:].astype(f32),
                    0.0,
                ),
                axis=1,
                keepdims=True,
            )
            out = jnp.dot(activated[i * n : (i + 1) * n], weight_out, preferred_element_type=f32)
            outs.append((out * weights).astype(bf16))
        back = scatter_far(*outs, far_axis).reshape(4, 4 * rows, half)
        sums.append(scatter_near(back, near_axis).astype(bf16))
    to_x = jnp.stack([s.reshape(4, rows, half) for s in sums], axis=1)
    chip_out = scatter_near(to_x, "x")

    attention_out = to_tokens(attention.reshape(2, rows, half))
    expert_sum = to_tokens(chip_out.astype(bf16))
    residual_mid = total(residual_in, attention_out).astype(bf16)
    layer_output = total(residual_mid, expert_sum).astype(bf16)
    return (attention_out, layer_output)


def solution(mesh):
    torus = Mesh(mesh.devices.reshape(4, 4, 4, 2), ("y", "z", "x", "core"))
    dp, tp = ("y", "z"), ("x", "core")
    both = dp + tp
    placed = (
        P(both, None),
        P(both, None, None),
        P(both, None, None),
        P(both, None),
        P(both),
        P(tp, None, None),
        P(tp, None),
        P(),
        P(both, None),
        P(both, None),
        P(),
        P(dp, None, None, tp),
        P(dp, tp, None),
    )
    return jax.shard_map(
        per_device,
        mesh=torus,
        in_specs=placed,
        out_specs=(P(both, None), P(both, None)),
        check_vma=False,
    )
```

```python
import jax
import jax.numpy as jnp
from jax import lax
from jax.sharding import Mesh, PartitionSpec as P

score_scale = 192.0 ** (-0.5)
route_scale = 2.5
norm_eps = 1e-06
f32 = jnp.float32
bf16 = jnp.bfloat16


def attend(query_rows, cache_rows, fresh_key, context_lengths, latent_width):
    scores = (
        jnp.einsum("rhc,rtc->rht", query_rows, cache_rows, preferred_element_type=jnp.float32)
        * score_scale
    )
    own_score = (
        jnp.einsum("rhc,rc->rh", query_rows, fresh_key, preferred_element_type=jnp.float32)
        * score_scale
    )
    positions = lax.broadcasted_iota(jnp.int32, scores.shape, 2)
    scores = jnp.where(positions < context_lengths[:, None, None], scores, -jnp.inf)
    row_max = jnp.maximum(jnp.max(scores, axis=2), own_score)
    cache_weights = jnp.exp(scores - row_max[:, :, None])
    own_weight = jnp.exp(own_score - row_max)
    denominator = jnp.sum(cache_weights, axis=2) + own_weight
    cache_weights = (cache_weights / denominator[:, :, None]).astype(jnp.bfloat16)
    own_weight = (own_weight / denominator).astype(jnp.bfloat16)
    own_weight = lax.optimization_barrier(own_weight).astype(jnp.float32)
    result = jnp.einsum(
        "rht,rtl->rhl",
        cache_weights,
        cache_rows[:, :, :latent_width],
        preferred_element_type=jnp.float32,
    )
    result = result + own_weight[:, :, None] * fresh_key[:, None, :latent_width].astype(jnp.float32)
    return result.astype(jnp.bfloat16)


def combine_table(expert_ids, gates, expert_slots):
    slot_count = expert_slots.shape[0]
    labels = lax.broadcasted_iota(jnp.int32, (1, 1, slot_count), 2)
    slot_of = jnp.sum(
        jnp.where(expert_ids[:, :, None] == labels, expert_slots[None, None, :], 0), axis=2
    )
    slot_hits = slot_of[:, :, None] == labels
    weight_table = jnp.sum(jnp.where(slot_hits, gates[:, :, None].astype(jnp.float32), 0.0), axis=1)
    return weight_table.astype(jnp.bfloat16)


near_axis = ("y", "z")
far_axis = ("z", "y")


def ring(axes, distance):
    pairs = []
    for y in range(4):
        for z in range(4):
            for core in range(2):
                if axes[core] == "y":
                    source = ((y + distance) % 4, z)
                else:
                    source = (y, (z + distance) % 4)
                pairs.append(((source[0] * 4 + source[1]) * 2 + core, (y * 4 + z) * 2 + core))
    return pairs


def shift(value, axes, distance):
    if axes == "x":
        return lax.ppermute(value, "x", [((i + distance) % 4, i) for i in range(4)])
    return lax.ppermute(value, ("y", "z", "core"), ring(axes, distance))


def swap(value):
    return lax.ppermute(value, "core", [(0, 1), (1, 0)])


def total(*terms):
    return sum(term.astype(f32) for term in terms)


def gather_near(block, axes):
    return jnp.stack([block, shift(block, axes, 1), shift(block, axes, 2), shift(block, axes, -1)])


def gather_far(block, axes):
    half = block.shape[0] // 2
    right, left = shift(block, axes, 1), shift(block, axes, -1)
    low, high = shift(right[:half], axes, 1), shift(left[half:], axes, -1)
    return [block, right, jnp.concatenate([low, high], axis=0), left]


def scatter_far(own, right, opposite, left, axes):
    half = own.shape[0] // 2
    low, high = shift(opposite[:half], axes, -1), shift(opposite[half:], axes, 1)
    right = jnp.concatenate([total(right[:half], low).astype(bf16), right[half:]], axis=0)
    left = jnp.concatenate([left[:half], total(left[half:], high).astype(bf16)], axis=0)
    return total(own, shift(right, axes, -1), shift(left, axes, 1)).astype(bf16)


def scatter_near(value, axes):
    return total(
        value[0], shift(value[1], axes, -1), shift(value[2], axes, 2), shift(value[3], axes, 1)
    )


def per_device(
    residual_in,
    query_latent,
    latent_cache,
    new_latent,
    context_lengths,
    value_up,
    out_proj,
    norm_gain,
    expert_ids,
    route_scores,
    expert_slots,
    expert_gate_up,
    expert_down,
):
    rows, model_width = residual_in.shape
    latent_width = value_up.shape[1]
    half = model_width // 2
    lanes = 128
    core = lax.axis_index("core")
    x_at = lax.axis_index("x")
    expert_at = lax.axis_index("y") * 4 + lax.axis_index("z")

    def mine(value, axis):
        return lax.dynamic_slice_in_dim(value, core * half, half, axis=axis)

    def others(value, axis):
        return lax.dynamic_slice_in_dim(value, (1 - core) * half, half, axis=axis)

    def by_core(own, got):
        return jnp.where(core == 0, jnp.stack([own, got]), jnp.stack([got, own]))

    def to_tokens(chip):
        own = jnp.where(core == 0, chip[0], chip[1])
        got = swap(jnp.where(core == 0, chip[1], chip[0]))
        return jnp.where(
            core == 0,
            jnp.concatenate([own, got], axis=1),
            jnp.concatenate([got, own], axis=1),
        )

    gates = (route_scale * route_scores / jnp.sum(route_scores, axis=1, keepdims=True)).astype(bf16)
    table = combine_table(expert_ids, gates, expert_slots)
    table = jnp.pad(table, ((0, 0), (0, lanes - table.shape[1])))

    latent_out = attend(query_latent, latent_cache, new_latent, context_lengths, latent_width)
    exchanged = lax.all_to_all(latent_out, ("x", "core"), split_axis=1, concat_axis=0, tiled=True)

    gate_up = expert_gate_up[0]
    down = expert_down[0]
    gate_up_own = mine(gate_up, 1)
    gate_up_got = swap(others(gate_up, 1))
    weight_in = jnp.concatenate(
        [gate_up_own[0], gate_up_own[1], gate_up_got[0], gate_up_got[1]], axis=1
    )
    weight_in = jnp.pad(weight_in, ((0, lanes), (0, 0)))
    weight_out = jnp.concatenate([mine(down, 1), swap(others(down, 1))], axis=0)

    chip_rows = by_core(
        jnp.concatenate([mine(residual_in, 1), table], axis=1),
        swap(jnp.concatenate([others(residual_in, 1), table], axis=1)),
    ).reshape(2 * rows, half + lanes)
    chip_residual, chip_table = chip_rows[:, :half], chip_rows[:, half:]

    values = jnp.einsum(
        "thl,hlv->thv", exchanged, value_up, preferred_element_type=f32
    ).astype(bf16)
    values = values.reshape(values.shape[0], values.shape[1] * values.shape[2])
    projected = jnp.dot(values, out_proj, preferred_element_type=f32)
    chip_sum = mine(projected, 1) + swap(others(projected, 1).astype(bf16)).astype(f32)
    chip_sum = chip_sum.reshape(4, 2 * rows, half)

    def for_chip(distance):
        place = lax.rem(x_at + distance, 4)
        return lax.dynamic_index_in_dim(chip_sum, place, axis=0, keepdims=False)

    attention = total(
        for_chip(0),
        shift(for_chip(1).astype(bf16), "x", -1),
        shift(for_chip(2).astype(bf16), "x", 2),
        shift(for_chip(3).astype(bf16), "x", 1),
    ).astype(bf16)
    residual_f32 = total(chip_residual, attention).astype(bf16).astype(f32)
    squares = jnp.sum(residual_f32 * residual_f32, axis=1, keepdims=True)
    squares = squares + swap(squares)
    scaling = lax.rsqrt(squares / model_width + norm_eps)
    gain = mine(norm_gain, 0).astype(f32)
    normed = (residual_f32 * scaling * gain[None, :]).astype(bf16)
    payload = jnp.concatenate([normed, chip_table], axis=1)

    width = half + lanes
    group = gather_near(payload, "x").reshape(8 * rows, width)
    count = 8 * rows

    far_own = gather_far(group, far_axis)
    right, left, opposite = (shift(group, near_axis, d) for d in (1, -1, 2))
    far_sides = gather_far(jnp.concatenate([right, left], axis=0), far_axis)
    far_opposite = gather_far(opposite, far_axis)

    hidden = weight_in.shape[1] // 2
    units = hidden // 2

    def crossed(value):
        value = value.reshape(4, 4, count, value.shape[1])
        return value.transpose(1, 0, 2, 3).reshape(16 * count, value.shape[3])

    def into(blocks):
        return [jnp.dot(b, weight_in, preferred_element_type=f32) for b in blocks]

    def table_of(blocks):
        labels = lax.broadcasted_iota(jnp.int32, (1, lanes), 1)
        return [
            jnp.sum(
                jnp.where(labels == expert_at, b[:, half:].astype(f32), 0.0), axis=1, keepdims=True
            )
            for b in blocks
        ]

    def by_near(own, sides, opposite):
        return jnp.concatenate(
            own + [v[:count] for v in sides] + opposite + [v[count:] for v in sides], axis=0
        )

    product = by_near(into(far_own), into(far_sides), into(far_opposite))
    weights = by_near(table_of(far_own), table_of(far_sides), table_of(far_opposite))
    got = swap(product[:, hidden:].astype(bf16))
    product = product[:, :hidden] + crossed(got).astype(f32)
    activated = (jax.nn.silu(product[:, :units]) * product[:, units:]).astype(bf16)
    activated = jnp.concatenate([activated, crossed(swap(activated))], axis=1)

    def out_of(near):
        rows_of = slice(near * 4 * count, (near + 1) * 4 * count)
        out = jnp.dot(activated[rows_of], weight_out, preferred_element_type=f32)
        out = (out * weights[rows_of]).astype(bf16)
        return [out[i * count : (i + 1) * count] for i in range(4)]

    back_opposite = scatter_far(*out_of(2), far_axis)
    sides = [jnp.concatenate(pair, axis=0) for pair in zip(out_of(1), out_of(3))]
    back_sides = scatter_far(*sides, far_axis)
    back_own = scatter_far(*out_of(0), far_axis)
    summed = total(
        back_own,
        shift(back_sides[:count], near_axis, -1),
        shift(back_opposite, near_axis, 2),
        shift(back_sides[count:], near_axis, 1),
    ).astype(bf16)
    to_x = summed.reshape(4, 2, rows, half)
    chip_out = scatter_near(to_x, "x")

    attention_out = to_tokens(attention.reshape(2, rows, half))
    expert_sum = to_tokens(chip_out.astype(bf16))
    residual_mid = total(residual_in, attention_out).astype(bf16)
    layer_output = total(residual_mid, expert_sum).astype(bf16)
    return (attention_out, layer_output)


def solution(mesh):
    torus = Mesh(mesh.devices.reshape(4, 4, 4, 2), ("y", "z", "x", "core"))
    dp, tp = ("y", "z"), ("x", "core")
    both = dp + tp
    placed = (
        P(both, None),
        P(both, None, None),
        P(both, None, None),
        P(both, None),
        P(both),
        P(tp, None, None),
        P(tp, None),
        P(),
        P(both, None),
        P(both, None),
        P(),
        P(dp, None, None, tp),
        P(dp, tp, None),
    )
    return jax.shard_map(
        per_device,
        mesh=torus,
        in_specs=placed,
        out_specs=(P(both, None), P(both, None)),
        check_vma=False,
    )
```

```python
import jax
import jax.numpy as jnp
from jax import lax
from jax.experimental import pallas as pl
from jax.experimental.pallas import tpu as pltpu
from jax.sharding import Mesh, PartitionSpec as P

score_scale = 192.0 ** (-0.5)
route_scale = 2.5
norm_eps = 1e-06
f32 = jnp.float32
bf16 = jnp.bfloat16


def attend(query_rows, cache_rows, fresh_key, context_lengths, latent_width):
    scores = (
        jnp.einsum("rhc,rtc->rht", query_rows, cache_rows, preferred_element_type=jnp.float32)
        * score_scale
    )
    own_score = (
        jnp.einsum("rhc,rc->rh", query_rows, fresh_key, preferred_element_type=jnp.float32)
        * score_scale
    )
    positions = lax.broadcasted_iota(jnp.int32, scores.shape, 2)
    scores = jnp.where(positions < context_lengths[:, None, None], scores, -jnp.inf)
    row_max = jnp.maximum(jnp.max(scores, axis=2), own_score)
    cache_weights = jnp.exp(scores - row_max[:, :, None])
    own_weight = jnp.exp(own_score - row_max)
    denominator = jnp.sum(cache_weights, axis=2) + own_weight
    cache_weights = (cache_weights / denominator[:, :, None]).astype(jnp.bfloat16)
    own_weight = (own_weight / denominator).astype(jnp.bfloat16)
    own_weight = lax.optimization_barrier(own_weight).astype(jnp.float32)
    result = jnp.einsum(
        "rht,rtl->rhl",
        cache_weights,
        cache_rows[:, :, :latent_width],
        preferred_element_type=jnp.float32,
    )
    result = result + own_weight[:, :, None] * fresh_key[:, None, :latent_width].astype(jnp.float32)
    return result.astype(jnp.bfloat16)


def combine_table(expert_ids, gates, expert_slots):
    slot_count = expert_slots.shape[0]
    labels = lax.broadcasted_iota(jnp.int32, (1, 1, slot_count), 2)
    slot_of = jnp.sum(
        jnp.where(expert_ids[:, :, None] == labels, expert_slots[None, None, :], 0), axis=2
    )
    slot_hits = slot_of[:, :, None] == labels
    weight_table = jnp.sum(jnp.where(slot_hits, gates[:, :, None].astype(jnp.float32), 0.0), axis=1)
    return weight_table.astype(jnp.bfloat16)


def project_block(first_ref, values_ref, weight_ref, out_ref):
    out_ref[...] = jnp.dot(values_ref[...], weight_ref[...], preferred_element_type=f32)


def project(values, weight, core):
    rows, depth = values.shape
    width = weight.shape[1]
    block = 512
    blocks = width // block
    first = ((1 - core) * (blocks // 2)).astype(jnp.int32).reshape(1)
    return pl.pallas_call(
        project_block,
        out_shape=jax.ShapeDtypeStruct((rows, width), f32),
        grid_spec=pltpu.PrefetchScalarGridSpec(
            num_scalar_prefetch=1,
            grid=(blocks,),
            in_specs=[
                pl.BlockSpec((rows, depth), lambda i, first: (0, 0)),
                pl.BlockSpec((depth, block), lambda i, first: (0, lax.rem(i + first[0], blocks))),
            ],
            out_specs=pl.BlockSpec((rows, block), lambda i, first: (0, i)),
        ),
        compiler_params=pltpu.CompilerParams(vmem_limit_bytes=16 * 1024 * 1024),
        cost_estimate=pl.CostEstimate(
            flops=2 * rows * depth * width, bytes_accessed=2 * depth * width, transcendentals=0
        ),
        name="project",
    )(first, values, weight)


near_axis = ("y", "z")
far_axis = ("z", "y")


def ring(axes, distance):
    pairs = []
    for y in range(4):
        for z in range(4):
            for core in range(2):
                if axes[core] == "y":
                    source = ((y + distance) % 4, z)
                else:
                    source = (y, (z + distance) % 4)
                pairs.append(((source[0] * 4 + source[1]) * 2 + core, (y * 4 + z) * 2 + core))
    return pairs


def shift(value, axes, distance):
    if axes == "x":
        return lax.ppermute(value, "x", [((i + distance) % 4, i) for i in range(4)])
    return lax.ppermute(value, ("y", "z", "core"), ring(axes, distance))


def swap(value):
    return lax.ppermute(value, "core", [(0, 1), (1, 0)])


def total(*terms):
    return sum(term.astype(f32) for term in terms)


def gather_near(block, axes):
    return jnp.stack([block, shift(block, axes, 1), shift(block, axes, 2), shift(block, axes, -1)])


def gather_far(block, axes):
    half = block.shape[0] // 2
    right, left = shift(block, axes, 1), shift(block, axes, -1)
    low, high = shift(right[:half], axes, 1), shift(left[half:], axes, -1)
    return [block, right, jnp.concatenate([low, high], axis=0), left]


def scatter_far(own, right, opposite, left, axes):
    half = own.shape[0] // 2
    low, high = shift(opposite[:half], axes, -1), shift(opposite[half:], axes, 1)
    right = jnp.concatenate([total(right[:half], low).astype(bf16), right[half:]], axis=0)
    left = jnp.concatenate([left[:half], total(left[half:], high).astype(bf16)], axis=0)
    return total(own, shift(right, axes, -1), shift(left, axes, 1)).astype(bf16)


def scatter_near(value, axes):
    return total(
        value[0], shift(value[1], axes, -1), shift(value[2], axes, 2), shift(value[3], axes, 1)
    )


def per_device(
    residual_in,
    query_latent,
    latent_cache,
    new_latent,
    context_lengths,
    value_up,
    out_proj,
    norm_gain,
    expert_ids,
    route_scores,
    expert_slots,
    expert_gate_up,
    expert_down,
):
    rows, model_width = residual_in.shape
    latent_width = value_up.shape[1]
    half = model_width // 2
    lanes = 128
    core = lax.axis_index("core")
    x_at = lax.axis_index("x")
    expert_at = lax.axis_index("y") * 4 + lax.axis_index("z")

    def mine(value, axis):
        return lax.dynamic_slice_in_dim(value, core * half, half, axis=axis)

    def others(value, axis):
        return lax.dynamic_slice_in_dim(value, (1 - core) * half, half, axis=axis)

    def by_core(own, got):
        return jnp.where(core == 0, jnp.stack([own, got]), jnp.stack([got, own]))

    def to_tokens(chip):
        own = jnp.where(core == 0, chip[0], chip[1])
        got = swap(jnp.where(core == 0, chip[1], chip[0]))
        return jnp.where(
            core == 0,
            jnp.concatenate([own, got], axis=1),
            jnp.concatenate([got, own], axis=1),
        )

    gates = (route_scale * route_scores / jnp.sum(route_scores, axis=1, keepdims=True)).astype(bf16)
    table = combine_table(expert_ids, gates, expert_slots)
    table = jnp.pad(table, ((0, 0), (0, lanes - table.shape[1])))

    latent_out = attend(query_latent, latent_cache, new_latent, context_lengths, latent_width)
    exchanged = lax.all_to_all(latent_out, ("x", "core"), split_axis=1, concat_axis=0, tiled=True)

    gate_up = expert_gate_up[0]
    down = expert_down[0]
    gate_up_own = mine(gate_up, 1)
    gate_up_got = swap(others(gate_up, 1))
    weight_in = jnp.concatenate(
        [gate_up_own[0], gate_up_own[1], gate_up_got[0], gate_up_got[1]], axis=1
    )
    weight_in = jnp.pad(weight_in, ((0, lanes), (0, 0)))
    weight_out = jnp.concatenate([mine(down, 1), swap(others(down, 1))], axis=0)

    chip_rows = by_core(
        jnp.concatenate([mine(residual_in, 1), table], axis=1),
        swap(jnp.concatenate([others(residual_in, 1), table], axis=1)),
    ).reshape(2 * rows, half + lanes)
    chip_residual, chip_table = chip_rows[:, :half], chip_rows[:, half:]

    values = jnp.einsum(
        "thl,hlv->thv", exchanged, value_up, preferred_element_type=f32
    ).astype(bf16)
    values = values.reshape(values.shape[0], values.shape[1] * values.shape[2])
    projected = project(values, out_proj, core)
    chip_sum = projected[:, half:] + swap(projected[:, :half].astype(bf16)).astype(f32)
    chip_sum = chip_sum.reshape(4, 2 * rows, half)

    def for_chip(distance):
        place = lax.rem(x_at + distance, 4)
        return lax.dynamic_index_in_dim(chip_sum, place, axis=0, keepdims=False)

    attention = total(
        for_chip(0),
        shift(for_chip(1).astype(bf16), "x", -1),
        shift(for_chip(2).astype(bf16), "x", 2),
        shift(for_chip(3).astype(bf16), "x", 1),
    ).astype(bf16)
    residual_f32 = total(chip_residual, attention).astype(bf16).astype(f32)
    squares = jnp.sum(residual_f32 * residual_f32, axis=1, keepdims=True)
    squares = squares + swap(squares)
    scaling = lax.rsqrt(squares / model_width + norm_eps)
    gain = mine(norm_gain, 0).astype(f32)
    normed = (residual_f32 * scaling * gain[None, :]).astype(bf16)
    payload = jnp.concatenate([normed, chip_table], axis=1)

    width = half + lanes
    group = gather_near(payload, "x").reshape(8 * rows, width)
    count = 8 * rows

    far_own = gather_far(group, far_axis)
    near = [shift(group, near_axis, d) for d in (1, 2, -1)]
    part = count // 2
    rest = [
        gather_far(jnp.concatenate([v[c * part : (c + 1) * part] for v in near], axis=0), far_axis)
        for c in range(2)
    ]

    hidden = weight_in.shape[1] // 2
    units = hidden // 2

    def crossed(value):
        value = value.reshape(4, 4, count, value.shape[1])
        return value.transpose(1, 0, 2, 3).reshape(16 * count, value.shape[3])

    def into(blocks):
        return [jnp.dot(b, weight_in, preferred_element_type=f32) for b in blocks]

    def table_of(blocks):
        labels = lax.broadcasted_iota(jnp.int32, (1, lanes), 1)
        return [
            jnp.sum(
                jnp.where(labels == expert_at, b[:, half:].astype(f32), 0.0), axis=1, keepdims=True
            )
            for b in blocks
        ]

    def in_order(own, rest):
        return jnp.concatenate(own + rest[0] + rest[1], axis=0)

    def by_near(value):
        cut = 4 * count
        own = value[:cut].reshape(1, 4, 2, part, value.shape[1])
        others = value[cut:].reshape(2, 4, 3, part, value.shape[1]).transpose(2, 1, 0, 3, 4)
        return jnp.concatenate([own, others], axis=0).reshape(16 * count, value.shape[1])

    def by_chunk(value):
        value = value.reshape(4, 4, 2, part, value.shape[1])
        own, others = value[:1], value[1:].transpose(2, 1, 0, 3, 4)
        return jnp.concatenate(
            [own.reshape(4 * count, value.shape[4]), others.reshape(12 * count, value.shape[4])],
            axis=0,
        )

    product = in_order(into(far_own), [into(r) for r in rest])
    weights = in_order(table_of(far_own), [table_of(r) for r in rest])
    got = swap(product[:, hidden:].astype(bf16))
    product = product[:, :hidden] + by_chunk(crossed(by_near(got))).astype(f32)
    activated = (jax.nn.silu(product[:, :units]) * product[:, units:]).astype(bf16)
    activated = jnp.concatenate([activated, by_chunk(crossed(by_near(swap(activated))))], axis=1)

    def out_of(start, size):
        rows_of = slice(start, start + 4 * size)
        out = jnp.dot(activated[rows_of], weight_out, preferred_element_type=f32)
        out = (out * weights[rows_of]).astype(bf16)
        return [out[i * size : (i + 1) * size] for i in range(4)]

    cut = 4 * count
    back = [scatter_far(*out_of(cut + c * 12 * part, 3 * part), far_axis) for c in range(2)]
    back_own = scatter_far(*out_of(0, count), far_axis)
    sent = [
        jnp.concatenate([b[n * part : (n + 1) * part] for b in back], axis=0) for n in range(3)
    ]
    summed = total(
        back_own,
        shift(sent[0], near_axis, -1),
        shift(sent[1], near_axis, 2),
        shift(sent[2], near_axis, 1),
    ).astype(bf16)
    to_x = summed.reshape(4, 2, rows, half)
    chip_out = scatter_near(to_x, "x")

    attention_out = to_tokens(attention.reshape(2, rows, half))
    expert_sum = to_tokens(chip_out.astype(bf16))
    residual_mid = total(residual_in, attention_out).astype(bf16)
    layer_output = total(residual_mid, expert_sum).astype(bf16)
    return (attention_out, layer_output)


def solution(mesh):
    torus = Mesh(mesh.devices.reshape(4, 4, 4, 2), ("y", "z", "x", "core"))
    dp, tp = ("y", "z"), ("x", "core")
    both = dp + tp
    placed = (
        P(both, None),
        P(both, None, None),
        P(both, None, None),
        P(both, None),
        P(both),
        P(tp, None, None),
        P(tp, None),
        P(),
        P(both, None),
        P(both, None),
        P(),
        P(dp, None, None, tp),
        P(dp, tp, None),
    )
    return jax.shard_map(
        per_device,
        mesh=torus,
        in_specs=placed,
        out_specs=(P(both, None), P(both, None)),
        check_vma=False,
    )
```

```python
import jax
import jax.numpy as jnp
from jax import lax
from jax.sharding import Mesh, PartitionSpec as P

score_scale = 192.0 ** (-0.5)
route_scale = 2.5
norm_eps = 1e-06
f32 = jnp.float32
bf16 = jnp.bfloat16


def attend(query_rows, cache_rows, fresh_key, context_lengths, latent_width):
    scores = (
        jnp.einsum("rhc,rtc->rht", query_rows, cache_rows, preferred_element_type=jnp.float32)
        * score_scale
    )
    own_score = (
        jnp.einsum("rhc,rc->rh", query_rows, fresh_key, preferred_element_type=jnp.float32)
        * score_scale
    )
    positions = lax.broadcasted_iota(jnp.int32, scores.shape, 2)
    scores = jnp.where(positions < context_lengths[:, None, None], scores, -jnp.inf)
    row_max = jnp.maximum(jnp.max(scores, axis=2), own_score)
    cache_weights = jnp.exp(scores - row_max[:, :, None])
    own_weight = jnp.exp(own_score - row_max)
    denominator = jnp.sum(cache_weights, axis=2) + own_weight
    cache_weights = (cache_weights / denominator[:, :, None]).astype(jnp.bfloat16)
    own_weight = (own_weight / denominator).astype(jnp.bfloat16)
    own_weight = lax.optimization_barrier(own_weight).astype(jnp.float32)
    result = jnp.einsum(
        "rht,rtl->rhl",
        cache_weights,
        cache_rows[:, :, :latent_width],
        preferred_element_type=jnp.float32,
    )
    result = result + own_weight[:, :, None] * fresh_key[:, None, :latent_width].astype(jnp.float32)
    return result.astype(jnp.bfloat16)


def combine_table(expert_ids, gates, expert_slots):
    slot_count = expert_slots.shape[0]
    labels = lax.broadcasted_iota(jnp.int32, (1, 1, slot_count), 2)
    slot_of = jnp.sum(
        jnp.where(expert_ids[:, :, None] == labels, expert_slots[None, None, :], 0), axis=2
    )
    slot_hits = slot_of[:, :, None] == labels
    weight_table = jnp.sum(jnp.where(slot_hits, gates[:, :, None].astype(jnp.float32), 0.0), axis=1)
    return weight_table.astype(jnp.bfloat16)


near_axis = ("y", "z")
far_axis = ("z", "y")


def ring(axes, distance):
    pairs = []
    for y in range(4):
        for z in range(4):
            for core in range(2):
                if axes[core] == "y":
                    source = ((y + distance) % 4, z)
                else:
                    source = (y, (z + distance) % 4)
                pairs.append(((source[0] * 4 + source[1]) * 2 + core, (y * 4 + z) * 2 + core))
    return pairs


def shift(value, axes, distance):
    if axes == "x":
        return lax.ppermute(value, "x", [((i + distance) % 4, i) for i in range(4)])
    return lax.ppermute(value, ("y", "z", "core"), ring(axes, distance))


def swap(value):
    return lax.ppermute(value, "core", [(0, 1), (1, 0)])


def total(*terms):
    return sum(term.astype(f32) for term in terms)


def gather_near(block, axes):
    return jnp.stack([block, shift(block, axes, 1), shift(block, axes, 2), shift(block, axes, -1)])


def gather_far(block, axes):
    half = block.shape[0] // 2
    right, left = shift(block, axes, 1), shift(block, axes, -1)
    low, high = shift(right[:half], axes, 1), shift(left[half:], axes, -1)
    return [block, right, jnp.concatenate([low, high], axis=0), left]


def scatter_far(own, right, opposite, left, axes):
    half = own.shape[0] // 2
    low, high = shift(opposite[:half], axes, -1), shift(opposite[half:], axes, 1)
    right = jnp.concatenate([total(right[:half], low).astype(bf16), right[half:]], axis=0)
    left = jnp.concatenate([left[:half], total(left[half:], high).astype(bf16)], axis=0)
    return total(own, shift(right, axes, -1), shift(left, axes, 1)).astype(bf16)


def scatter_near(value, axes):
    return total(
        value[0], shift(value[1], axes, -1), shift(value[2], axes, 2), shift(value[3], axes, 1)
    )


def per_device(
    residual_in,
    query_latent,
    latent_cache,
    new_latent,
    context_lengths,
    value_up,
    out_proj,
    norm_gain,
    expert_ids,
    route_scores,
    expert_slots,
    expert_gate_up,
    expert_down,
):
    rows, model_width = residual_in.shape
    latent_width = value_up.shape[1]
    half = model_width // 2
    lanes = 128
    core = lax.axis_index("core")
    x_at = lax.axis_index("x")
    expert_at = lax.axis_index("y") * 4 + lax.axis_index("z")

    def mine(value, axis):
        return lax.dynamic_slice_in_dim(value, core * half, half, axis=axis)

    def others(value, axis):
        return lax.dynamic_slice_in_dim(value, (1 - core) * half, half, axis=axis)

    def by_core(own, got):
        return jnp.where(core == 0, jnp.stack([own, got]), jnp.stack([got, own]))

    def to_tokens(chip):
        own = jnp.where(core == 0, chip[0], chip[1])
        got = swap(jnp.where(core == 0, chip[1], chip[0]))
        return jnp.where(
            core == 0,
            jnp.concatenate([own, got], axis=1),
            jnp.concatenate([got, own], axis=1),
        )

    gates = (route_scale * route_scores / jnp.sum(route_scores, axis=1, keepdims=True)).astype(bf16)
    table = combine_table(expert_ids, gates, expert_slots)
    table = jnp.pad(table, ((0, 0), (0, lanes - table.shape[1])))

    latent_out = attend(query_latent, latent_cache, new_latent, context_lengths, latent_width)
    exchanged = lax.all_to_all(latent_out, ("x", "core"), split_axis=1, concat_axis=0, tiled=True)

    gate_up = expert_gate_up[0]
    down = expert_down[0]
    gate_up_own = mine(gate_up, 1)
    gate_up_got = swap(others(gate_up, 1))
    weight_in = jnp.concatenate(
        [gate_up_own[0], gate_up_own[1], gate_up_got[0], gate_up_got[1]], axis=1
    )
    weight_in = jnp.pad(weight_in, ((0, lanes), (0, 0)))
    weight_out = jnp.concatenate([mine(down, 1), swap(others(down, 1))], axis=0)

    chip_rows = by_core(
        jnp.concatenate([mine(residual_in, 1), table], axis=1),
        swap(jnp.concatenate([others(residual_in, 1), table], axis=1)),
    ).reshape(2 * rows, half + lanes)
    chip_residual, chip_table = chip_rows[:, :half], chip_rows[:, half:]

    values = jnp.einsum(
        "thl,hlv->thv", exchanged, value_up, preferred_element_type=f32
    ).astype(bf16)
    values = values.reshape(values.shape[0], values.shape[1] * values.shape[2])
    projected = jnp.dot(values, out_proj, preferred_element_type=f32)
    chip_sum = mine(projected, 1) + swap(others(projected, 1).astype(bf16)).astype(f32)
    chip_sum = chip_sum.reshape(4, 2 * rows, half)

    def for_chip(distance):
        place = lax.rem(x_at + distance, 4)
        return lax.dynamic_index_in_dim(chip_sum, place, axis=0, keepdims=False)

    attention = total(
        for_chip(0),
        shift(for_chip(1).astype(bf16), "x", -1),
        shift(for_chip(2).astype(bf16), "x", 2),
        shift(for_chip(3).astype(bf16), "x", 1),
    ).astype(bf16)
    residual_f32 = total(chip_residual, attention).astype(bf16).astype(f32)
    squares = jnp.sum(residual_f32 * residual_f32, axis=1, keepdims=True)
    squares = squares + swap(squares)
    scaling = lax.rsqrt(squares / model_width + norm_eps)
    gain = mine(norm_gain, 0).astype(f32)
    normed = (residual_f32 * scaling * gain[None, :]).astype(bf16)
    payload = jnp.concatenate([normed, chip_table], axis=1)

    width = half + lanes
    group = gather_near(payload, "x").reshape(8 * rows, width)
    near = gather_near(group, near_axis).reshape(4, 4, 2, rows, width)

    chunks = [near[:, :, c].reshape(16 * rows, width) for c in range(2)]
    hidden = weight_in.shape[1] // 2
    units = hidden // 2

    def crossed(value):
        value = value.reshape(4, 4, 4 * rows, value.shape[1])
        return value.transpose(1, 0, 2, 3).reshape(64 * rows, value.shape[3])

    sums = []
    for chunk in chunks:
        blocks = gather_far(chunk, far_axis)
        products = [jnp.dot(b, weight_in, preferred_element_type=f32) for b in blocks]
        got = swap(jnp.concatenate([p[:, hidden:].astype(bf16) for p in products], axis=0))
        product = jnp.concatenate([p[:, :hidden] for p in products], axis=0)
        product = product + crossed(got).astype(f32)
        activated = (jax.nn.silu(product[:, :units]) * product[:, units:]).astype(bf16)
        activated = jnp.concatenate([activated, crossed(swap(activated))], axis=1)
        labels = lax.broadcasted_iota(jnp.int32, (1, lanes), 1)
        weights = jnp.concatenate(
            [
                jnp.sum(
                    jnp.where(labels == expert_at, b[:, half:].astype(f32), 0.0),
                    axis=1,
                    keepdims=True,
                )
                for b in blocks
            ],
            axis=0,
        )
        out = jnp.dot(activated, weight_out, preferred_element_type=f32)
        out = (out * weights).astype(bf16)
        n = 16 * rows
        outs = [out[i * n : (i + 1) * n] for i in range(4)]
        back = scatter_far(*outs, far_axis).reshape(4, 4 * rows, half)
        sums.append(scatter_near(back, near_axis).astype(bf16))
    to_x = jnp.stack([s.reshape(4, rows, half) for s in sums], axis=1)
    chip_out = scatter_near(to_x, "x")

    attention_out = to_tokens(attention.reshape(2, rows, half))
    expert_sum = to_tokens(chip_out.astype(bf16))
    residual_mid = total(residual_in, attention_out).astype(bf16)
    layer_output = total(residual_mid, expert_sum).astype(bf16)
    return (attention_out, layer_output)


def solution(mesh):
    torus = Mesh(mesh.devices.reshape(4, 4, 4, 2), ("y", "z", "x", "core"))
    dp, tp = ("y", "z"), ("x", "core")
    both = dp + tp
    placed = (
        P(both, None),
        P(both, None, None),
        P(both, None, None),
        P(both, None),
        P(both),
        P(tp, None, None),
        P(tp, None),
        P(),
        P(both, None),
        P(both, None),
        P(),
        P(dp, None, None, tp),
        P(dp, tp, None),
    )
    return jax.shard_map(
        per_device,
        mesh=torus,
        in_specs=placed,
        out_specs=(P(both, None), P(both, None)),
        check_vma=False,
    )
```

```python
import jax
import jax.numpy as jnp
from jax import lax
from jax.sharding import Mesh, PartitionSpec as P

score_scale = 192.0 ** (-0.5)
route_scale = 2.5
norm_eps = 1e-06
f32 = jnp.float32
bf16 = jnp.bfloat16


def attend(query_rows, cache_rows, fresh_key, context_lengths, latent_width):
    scores = (
        jnp.einsum("rhc,rtc->rht", query_rows, cache_rows, preferred_element_type=jnp.float32)
        * score_scale
    )
    own_score = (
        jnp.einsum("rhc,rc->rh", query_rows, fresh_key, preferred_element_type=jnp.float32)
        * score_scale
    )
    positions = lax.broadcasted_iota(jnp.int32, scores.shape, 2)
    scores = jnp.where(positions < context_lengths[:, None, None], scores, -jnp.inf)
    row_max = jnp.maximum(jnp.max(scores, axis=2), own_score)
    cache_weights = jnp.exp(scores - row_max[:, :, None])
    own_weight = jnp.exp(own_score - row_max)
    denominator = jnp.sum(cache_weights, axis=2) + own_weight
    cache_weights = (cache_weights / denominator[:, :, None]).astype(jnp.bfloat16)
    own_weight = (own_weight / denominator).astype(jnp.bfloat16)
    own_weight = lax.optimization_barrier(own_weight).astype(jnp.float32)
    result = jnp.einsum(
        "rht,rtl->rhl",
        cache_weights,
        cache_rows[:, :, :latent_width],
        preferred_element_type=jnp.float32,
    )
    result = result + own_weight[:, :, None] * fresh_key[:, None, :latent_width].astype(jnp.float32)
    return result.astype(jnp.bfloat16)


def combine_table(expert_ids, gates, expert_slots):
    slot_count = expert_slots.shape[0]
    labels = lax.broadcasted_iota(jnp.int32, (1, 1, slot_count), 2)
    slot_of = jnp.sum(
        jnp.where(expert_ids[:, :, None] == labels, expert_slots[None, None, :], 0), axis=2
    )
    slot_hits = slot_of[:, :, None] == labels
    weight_table = jnp.sum(jnp.where(slot_hits, gates[:, :, None].astype(jnp.float32), 0.0), axis=1)
    return weight_table.astype(jnp.bfloat16)


first_axis = ("x", "z")
near_axis = ("y", "x")
far_axis = ("z", "y")


def ring(axes, distance):
    pairs = []
    for target in range(128):
        core, place = target % 2, {"x": target // 2 % 4, "z": target // 8 % 4, "y": target // 32}
        place[axes[core]] = (place[axes[core]] + distance) % 4
        source = ((place["y"] * 4 + place["z"]) * 4 + place["x"]) * 2 + core
        pairs.append((source, target))
    return pairs


def shift(value, axes, distance):
    return lax.ppermute(value, ("y", "z", "x", "core"), ring(axes, distance))


def swap(value):
    return lax.ppermute(value, "core", [(0, 1), (1, 0)])


def total(*terms):
    return sum(term.astype(f32) for term in terms)


def gather_near(block, axes):
    return jnp.stack([block, shift(block, axes, 1), shift(block, axes, 2), shift(block, axes, -1)])


def gather_far(block, axes):
    half = block.shape[0] // 2
    right, left = shift(block, axes, 1), shift(block, axes, -1)
    low, high = shift(right[:half], axes, 1), shift(left[half:], axes, -1)
    return [block, right, jnp.concatenate([low, high], axis=0), left]


def scatter_far(own, right, opposite, left, axes):
    half = own.shape[0] // 2
    low, high = shift(opposite[:half], axes, -1), shift(opposite[half:], axes, 1)
    right = jnp.concatenate([total(right[:half], low).astype(bf16), right[half:]], axis=0)
    left = jnp.concatenate([left[:half], total(left[half:], high).astype(bf16)], axis=0)
    return total(own, shift(right, axes, -1), shift(left, axes, 1)).astype(bf16)


def scatter_near(value, axes):
    return total(
        value[0], shift(value[1], axes, -1), shift(value[2], axes, 2), shift(value[3], axes, 1)
    )


def per_device(
    residual_in,
    query_latent,
    latent_cache,
    new_latent,
    context_lengths,
    value_up,
    out_proj,
    norm_gain,
    expert_ids,
    route_scores,
    expert_slots,
    expert_gate_up,
    expert_down,
):
    rows, model_width = residual_in.shape
    latent_width = value_up.shape[1]
    half = model_width // 2
    lanes = 128
    core = lax.axis_index("core")
    x_at = lax.axis_index("x")
    expert_at = lax.axis_index("y") * 4 + lax.axis_index("z")

    def mine(value, axis):
        return lax.dynamic_slice_in_dim(value, core * half, half, axis=axis)

    def others(value, axis):
        return lax.dynamic_slice_in_dim(value, (1 - core) * half, half, axis=axis)

    def by_core(own, got):
        return jnp.where(core == 0, jnp.stack([own, got]), jnp.stack([got, own]))

    def to_tokens(chip):
        own = jnp.where(core == 0, chip[0], chip[1])
        got = swap(jnp.where(core == 0, chip[1], chip[0]))
        return jnp.where(
            core == 0,
            jnp.concatenate([own, got], axis=1),
            jnp.concatenate([got, own], axis=1),
        )

    gates = (route_scale * route_scores / jnp.sum(route_scores, axis=1, keepdims=True)).astype(bf16)
    table = combine_table(expert_ids, gates, expert_slots)
    table = jnp.pad(table, ((0, 0), (0, lanes - table.shape[1])))

    latent_out = attend(query_latent, latent_cache, new_latent, context_lengths, latent_width)
    exchanged = lax.all_to_all(latent_out, ("x", "core"), split_axis=1, concat_axis=0, tiled=True)

    gate_up = expert_gate_up[0]
    down = expert_down[0]
    gate_up_own = mine(gate_up, 1)
    gate_up_got = swap(others(gate_up, 1))
    weight_in = jnp.concatenate(
        [gate_up_own[0], gate_up_own[1], gate_up_got[0], gate_up_got[1]], axis=1
    )
    weight_in = jnp.pad(weight_in, ((0, lanes), (0, 0)))
    weight_out = jnp.concatenate([mine(down, 1), swap(others(down, 1))], axis=0)

    chip_rows = by_core(
        jnp.concatenate([mine(residual_in, 1), table], axis=1),
        swap(jnp.concatenate([others(residual_in, 1), table], axis=1)),
    ).reshape(2 * rows, half + lanes)
    chip_residual, chip_table = chip_rows[:, :half], chip_rows[:, half:]

    values = jnp.einsum(
        "thl,hlv->thv", exchanged, value_up, preferred_element_type=f32
    ).astype(bf16)
    values = values.reshape(values.shape[0], values.shape[1] * values.shape[2])
    projected = jnp.dot(values, out_proj, preferred_element_type=f32)
    chip_sum = mine(projected, 1) + swap(others(projected, 1).astype(bf16)).astype(f32)
    chip_sum = chip_sum.reshape(4, 2 * rows, half)

    def for_chip(distance):
        place = lax.rem(x_at + distance, 4)
        return lax.dynamic_index_in_dim(chip_sum, place, axis=0, keepdims=False)

    attention = total(
        for_chip(0),
        shift(for_chip(1).astype(bf16), ("x", "x"), -1),
        shift(for_chip(2).astype(bf16), ("x", "x"), 2),
        shift(for_chip(3).astype(bf16), ("x", "x"), 1),
    ).astype(bf16)
    residual_f32 = total(chip_residual, attention).astype(bf16).astype(f32)
    squares = jnp.sum(residual_f32 * residual_f32, axis=1, keepdims=True)
    squares = squares + swap(squares)
    scaling = lax.rsqrt(squares / model_width + norm_eps)
    gain = mine(norm_gain, 0).astype(f32)
    normed = (residual_f32 * scaling * gain[None, :]).astype(bf16)
    payload = jnp.concatenate([normed, chip_table], axis=1)

    width = half + lanes
    group = gather_near(payload, first_axis).reshape(8 * rows, width)
    near = gather_near(group, near_axis).reshape(4, 4, 2, rows, width)

    chunks = [near[:, :, c].reshape(16 * rows, width) for c in range(2)]
    hidden = weight_in.shape[1] // 2
    units = hidden // 2

    def crossed(value):
        value = value.reshape(4, 4, 4, rows, value.shape[1])
        value = jnp.where(
            core == 0, value.transpose(2, 0, 1, 3, 4), value.transpose(1, 2, 0, 3, 4)
        )
        return value.reshape(64 * rows, value.shape[4])

    sums = []
    for chunk in chunks:
        blocks = gather_far(chunk, far_axis)
        products = [jnp.dot(b, weight_in, preferred_element_type=f32) for b in blocks]
        got = swap(jnp.concatenate([p[:, hidden:].astype(bf16) for p in products], axis=0))
        product = jnp.concatenate([p[:, :hidden] for p in products], axis=0)
        product = product + crossed(got).astype(f32)
        activated = (jax.nn.silu(product[:, :units]) * product[:, units:]).astype(bf16)
        activated = jnp.concatenate([activated, crossed(swap(activated))], axis=1)
        labels = lax.broadcasted_iota(jnp.int32, (1, lanes), 1)
        weights = jnp.concatenate(
            [
                jnp.sum(
                    jnp.where(labels == expert_at, b[:, half:].astype(f32), 0.0),
                    axis=1,
                    keepdims=True,
                )
                for b in blocks
            ],
            axis=0,
        )
        out = jnp.dot(activated, weight_out, preferred_element_type=f32)
        out = (out * weights).astype(bf16)
        n = 16 * rows
        outs = [out[i * n : (i + 1) * n] for i in range(4)]
        back = scatter_far(*outs, far_axis).reshape(4, 4 * rows, half)
        sums.append(scatter_near(back, near_axis).astype(bf16))
    to_x = jnp.stack([s.reshape(4, rows, half) for s in sums], axis=1)
    chip_out = scatter_near(to_x, first_axis)

    attention_out = to_tokens(attention.reshape(2, rows, half))
    expert_sum = to_tokens(chip_out.astype(bf16))
    residual_mid = total(residual_in, attention_out).astype(bf16)
    layer_output = total(residual_mid, expert_sum).astype(bf16)
    return (attention_out, layer_output)


def solution(mesh):
    torus = Mesh(mesh.devices.reshape(4, 4, 4, 2), ("y", "z", "x", "core"))
    dp, tp = ("y", "z"), ("x", "core")
    both = dp + tp
    placed = (
        P(both, None),
        P(both, None, None),
        P(both, None, None),
        P(both, None),
        P(both),
        P(tp, None, None),
        P(tp, None),
        P(),
        P(both, None),
        P(both, None),
        P(),
        P(dp, None, None, tp),
        P(dp, tp, None),
    )
    return jax.shard_map(
        per_device,
        mesh=torus,
        in_specs=placed,
        out_specs=(P(both, None), P(both, None)),
        check_vma=False,
    )
```

```python
import jax
import jax.numpy as jnp
from jax import lax
from jax.sharding import Mesh, PartitionSpec as P

score_scale = 192.0 ** (-0.5)
route_scale = 2.5
norm_eps = 1e-06
f32 = jnp.float32
bf16 = jnp.bfloat16


def attend(query_rows, cache_rows, fresh_key, context_lengths, latent_width):
    scores = (
        jnp.einsum("rhc,rtc->rht", query_rows, cache_rows, preferred_element_type=jnp.float32)
        * score_scale
    )
    own_score = (
        jnp.einsum("rhc,rc->rh", query_rows, fresh_key, preferred_element_type=jnp.float32)
        * score_scale
    )
    positions = lax.broadcasted_iota(jnp.int32, scores.shape, 2)
    scores = jnp.where(positions < context_lengths[:, None, None], scores, -jnp.inf)
    row_max = jnp.maximum(jnp.max(scores, axis=2), own_score)
    cache_weights = jnp.exp(scores - row_max[:, :, None])
    own_weight = jnp.exp(own_score - row_max)
    denominator = jnp.sum(cache_weights, axis=2) + own_weight
    cache_weights = (cache_weights / denominator[:, :, None]).astype(jnp.bfloat16)
    own_weight = (own_weight / denominator).astype(jnp.bfloat16)
    own_weight = lax.optimization_barrier(own_weight).astype(jnp.float32)
    result = jnp.einsum(
        "rht,rtl->rhl",
        cache_weights,
        cache_rows[:, :, :latent_width],
        preferred_element_type=jnp.float32,
    )
    result = result + own_weight[:, :, None] * fresh_key[:, None, :latent_width].astype(jnp.float32)
    return result.astype(jnp.bfloat16)


def combine_table(expert_ids, gates, expert_slots):
    slot_count = expert_slots.shape[0]
    labels = lax.broadcasted_iota(jnp.int32, (1, 1, slot_count), 2)
    slot_of = jnp.sum(
        jnp.where(expert_ids[:, :, None] == labels, expert_slots[None, None, :], 0), axis=2
    )
    slot_hits = slot_of[:, :, None] == labels
    weight_table = jnp.sum(jnp.where(slot_hits, gates[:, :, None].astype(jnp.float32), 0.0), axis=1)
    return weight_table.astype(jnp.bfloat16)


first_axis = ("x", "z")
near_axis = ("y", "x")
far_axis = ("z", "y")


def ring(axes, distance):
    pairs = []
    for target in range(128):
        core, place = target % 2, {"x": target // 2 % 4, "z": target // 8 % 4, "y": target // 32}
        place[axes[core]] = (place[axes[core]] + distance) % 4
        source = ((place["y"] * 4 + place["z"]) * 4 + place["x"]) * 2 + core
        pairs.append((source, target))
    return pairs


def shift(value, axes, distance):
    return lax.ppermute(value, ("y", "z", "x", "core"), ring(axes, distance))


def swap(value):
    return lax.ppermute(value, "core", [(0, 1), (1, 0)])


def total(*terms):
    return sum(term.astype(f32) for term in terms)


def gather_near(block, axes):
    return jnp.stack([block, shift(block, axes, 1), shift(block, axes, 2), shift(block, axes, -1)])


def gather_far(block, axes):
    half = block.shape[0] // 2
    right, left = shift(block, axes, 1), shift(block, axes, -1)
    low, high = shift(right[:half], axes, 1), shift(left[half:], axes, -1)
    return [block, right, jnp.concatenate([low, high], axis=0), left]


def scatter_far(own, right, opposite, left, axes):
    half = own.shape[0] // 2
    low, high = shift(opposite[:half], axes, -1), shift(opposite[half:], axes, 1)
    right = jnp.concatenate([total(right[:half], low).astype(bf16), right[half:]], axis=0)
    left = jnp.concatenate([left[:half], total(left[half:], high).astype(bf16)], axis=0)
    return total(own, shift(right, axes, -1), shift(left, axes, 1)).astype(bf16)


def scatter_near(value, axes):
    return total(
        value[0], shift(value[1], axes, -1), shift(value[2], axes, 2), shift(value[3], axes, 1)
    )


def per_device(
    residual_in,
    query_latent,
    latent_cache,
    new_latent,
    context_lengths,
    value_up,
    out_proj,
    norm_gain,
    expert_ids,
    route_scores,
    expert_slots,
    expert_gate_up,
    expert_down,
):
    rows, model_width = residual_in.shape
    latent_width = value_up.shape[1]
    half = model_width // 2
    lanes = 128
    core = lax.axis_index("core")
    x_at = lax.axis_index("x")
    expert_at = lax.axis_index("y") * 4 + lax.axis_index("z")

    def mine(value, axis):
        return lax.dynamic_slice_in_dim(value, core * half, half, axis=axis)

    def others(value, axis):
        return lax.dynamic_slice_in_dim(value, (1 - core) * half, half, axis=axis)

    def by_core(own, got):
        return jnp.where(core == 0, jnp.stack([own, got]), jnp.stack([got, own]))

    def to_tokens(chip):
        own = jnp.where(core == 0, chip[0], chip[1])
        got = swap(jnp.where(core == 0, chip[1], chip[0]))
        return jnp.where(
            core == 0,
            jnp.concatenate([own, got], axis=1),
            jnp.concatenate([got, own], axis=1),
        )

    gates = (route_scale * route_scores / jnp.sum(route_scores, axis=1, keepdims=True)).astype(bf16)
    table = combine_table(expert_ids, gates, expert_slots)
    table = jnp.pad(table, ((0, 0), (0, lanes - table.shape[1])))

    latent_out = attend(query_latent, latent_cache, new_latent, context_lengths, latent_width)
    exchanged = lax.all_to_all(latent_out, ("x", "core"), split_axis=1, concat_axis=0, tiled=True)

    exchanged, expert_gate_up, expert_down = lax.optimization_barrier(
        (exchanged, expert_gate_up, expert_down)
    )
    gate_up = expert_gate_up[0]
    down = expert_down[0]
    gate_up_own = mine(gate_up, 1)
    gate_up_got = swap(others(gate_up, 1))
    weight_in = jnp.concatenate(
        [gate_up_own[0], gate_up_own[1], gate_up_got[0], gate_up_got[1]], axis=1
    )
    weight_in = jnp.pad(weight_in, ((0, lanes), (0, 0)))
    weight_out = jnp.concatenate([mine(down, 1), swap(others(down, 1))], axis=0)

    chip_rows = by_core(
        jnp.concatenate([mine(residual_in, 1), table], axis=1),
        swap(jnp.concatenate([others(residual_in, 1), table], axis=1)),
    ).reshape(2 * rows, half + lanes)
    chip_residual, chip_table = chip_rows[:, :half], chip_rows[:, half:]

    values = jnp.einsum(
        "thl,hlv->thv", exchanged, value_up, preferred_element_type=f32
    ).astype(bf16)
    values = values.reshape(values.shape[0], values.shape[1] * values.shape[2])
    projected = jnp.dot(values, out_proj, preferred_element_type=f32)
    chip_sum = mine(projected, 1) + swap(others(projected, 1).astype(bf16)).astype(f32)
    chip_sum = chip_sum.reshape(4, 2 * rows, half)

    def for_chip(distance):
        place = lax.rem(x_at + distance, 4)
        return lax.dynamic_index_in_dim(chip_sum, place, axis=0, keepdims=False)

    attention = total(
        for_chip(0),
        shift(for_chip(1).astype(bf16), ("x", "x"), -1),
        shift(for_chip(2).astype(bf16), ("x", "x"), 2),
        shift(for_chip(3).astype(bf16), ("x", "x"), 1),
    ).astype(bf16)
    residual_f32 = total(chip_residual, attention).astype(bf16).astype(f32)
    squares = jnp.sum(residual_f32 * residual_f32, axis=1, keepdims=True)
    squares = squares + swap(squares)
    scaling = lax.rsqrt(squares / model_width + norm_eps)
    gain = mine(norm_gain, 0).astype(f32)
    normed = (residual_f32 * scaling * gain[None, :]).astype(bf16)
    payload = jnp.concatenate([normed, chip_table], axis=1)

    width = half + lanes
    group = gather_near(payload, first_axis).reshape(8 * rows, width)
    near = gather_near(group, near_axis).reshape(4, 4, 2, rows, width)

    chunks = [near[:, :, c].reshape(16 * rows, width) for c in range(2)]
    hidden = weight_in.shape[1] // 2
    units = hidden // 2

    def crossed(value):
        value = value.reshape(4, 4, 4, rows, value.shape[1])
        value = jnp.where(
            core == 0, value.transpose(2, 0, 1, 3, 4), value.transpose(1, 2, 0, 3, 4)
        )
        return value.reshape(64 * rows, value.shape[4])

    sums = []
    for chunk in chunks:
        blocks = gather_far(chunk, far_axis)
        products = [jnp.dot(b, weight_in, preferred_element_type=f32) for b in blocks]
        got = swap(jnp.concatenate([p[:, hidden:].astype(bf16) for p in products], axis=0))
        product = jnp.concatenate([p[:, :hidden] for p in products], axis=0)
        product = product + crossed(got).astype(f32)
        activated = (jax.nn.silu(product[:, :units]) * product[:, units:]).astype(bf16)
        activated = jnp.concatenate([activated, crossed(swap(activated))], axis=1)
        labels = lax.broadcasted_iota(jnp.int32, (1, lanes), 1)
        weights = jnp.concatenate(
            [
                jnp.sum(
                    jnp.where(labels == expert_at, b[:, half:].astype(f32), 0.0),
                    axis=1,
                    keepdims=True,
                )
                for b in blocks
            ],
            axis=0,
        )
        out = jnp.dot(activated, weight_out, preferred_element_type=f32)
        out = (out * weights).astype(bf16)
        n = 16 * rows
        outs = [out[i * n : (i + 1) * n] for i in range(4)]
        back = scatter_far(*outs, far_axis).reshape(4, 4 * rows, half)
        sums.append(scatter_near(back, near_axis).astype(bf16))
    to_x = jnp.stack([s.reshape(4, rows, half) for s in sums], axis=1)
    chip_out = scatter_near(to_x, first_axis)

    attention_out = to_tokens(attention.reshape(2, rows, half))
    expert_sum = to_tokens(chip_out.astype(bf16))
    residual_mid = total(residual_in, attention_out).astype(bf16)
    layer_output = total(residual_mid, expert_sum).astype(bf16)
    return (attention_out, layer_output)


def solution(mesh):
    torus = Mesh(mesh.devices.reshape(4, 4, 4, 2), ("y", "z", "x", "core"))
    dp, tp = ("y", "z"), ("x", "core")
    both = dp + tp
    placed = (
        P(both, None),
        P(both, None, None),
        P(both, None, None),
        P(both, None),
        P(both),
        P(tp, None, None),
        P(tp, None),
        P(),
        P(both, None),
        P(both, None),
        P(),
        P(dp, None, None, tp),
        P(dp, tp, None),
    )
    return jax.shard_map(
        per_device,
        mesh=torus,
        in_specs=placed,
        out_specs=(P(both, None), P(both, None)),
        check_vma=False,
    )
```

```python
import jax
import jax.numpy as jnp
from jax import lax
from jax.sharding import Mesh, PartitionSpec as P

score_scale = 192.0 ** (-0.5)
route_scale = 2.5
norm_eps = 1e-06
f32 = jnp.float32
bf16 = jnp.bfloat16


def attend(query_rows, cache_rows, fresh_key, context_lengths, latent_width):
    scores = (
        jnp.einsum("rhc,rtc->rht", query_rows, cache_rows, preferred_element_type=jnp.float32)
        * score_scale
    )
    own_score = (
        jnp.einsum("rhc,rc->rh", query_rows, fresh_key, preferred_element_type=jnp.float32)
        * score_scale
    )
    positions = lax.broadcasted_iota(jnp.int32, scores.shape, 2)
    scores = jnp.where(positions < context_lengths[:, None, None], scores, -jnp.inf)
    row_max = jnp.maximum(jnp.max(scores, axis=2), own_score)
    cache_weights = jnp.exp(scores - row_max[:, :, None])
    own_weight = jnp.exp(own_score - row_max)
    denominator = jnp.sum(cache_weights, axis=2) + own_weight
    cache_weights = (cache_weights / denominator[:, :, None]).astype(jnp.bfloat16)
    own_weight = (own_weight / denominator).astype(jnp.bfloat16)
    own_weight = lax.optimization_barrier(own_weight).astype(jnp.float32)
    result = jnp.einsum(
        "rht,rtl->rhl",
        cache_weights,
        cache_rows[:, :, :latent_width],
        preferred_element_type=jnp.float32,
    )
    result = result + own_weight[:, :, None] * fresh_key[:, None, :latent_width].astype(jnp.float32)
    return result.astype(jnp.bfloat16)


def combine_table(expert_ids, gates, expert_slots):
    slot_count = expert_slots.shape[0]
    labels = lax.broadcasted_iota(jnp.int32, (1, 1, slot_count), 2)
    slot_of = jnp.sum(
        jnp.where(expert_ids[:, :, None] == labels, expert_slots[None, None, :], 0), axis=2
    )
    slot_hits = slot_of[:, :, None] == labels
    weight_table = jnp.sum(jnp.where(slot_hits, gates[:, :, None].astype(jnp.float32), 0.0), axis=1)
    return weight_table.astype(jnp.bfloat16)


first_axis = ("x", "z")
near_axis = ("y", "x")
far_axis = ("z", "y")


def ring(axes, distance):
    pairs = []
    for target in range(128):
        core, place = target % 2, {"x": target // 2 % 4, "z": target // 8 % 4, "y": target // 32}
        place[axes[core]] = (place[axes[core]] + distance) % 4
        source = ((place["y"] * 4 + place["z"]) * 4 + place["x"]) * 2 + core
        pairs.append((source, target))
    return pairs


def shift(value, axes, distance):
    return lax.ppermute(value, ("y", "z", "x", "core"), ring(axes, distance))


def swap(value):
    return lax.ppermute(value, "core", [(0, 1), (1, 0)])


def total(*terms):
    return sum(term.astype(f32) for term in terms)


def gather_near(block, axes):
    return jnp.stack([block, shift(block, axes, 1), shift(block, axes, 2), shift(block, axes, -1)])


def gather_far(block, axes):
    half = block.shape[0] // 2
    right, left = shift(block, axes, 1), shift(block, axes, -1)
    low, high = shift(right[:half], axes, 1), shift(left[half:], axes, -1)
    return [block, right, jnp.concatenate([low, high], axis=0), left]


def scatter_far(own, right, opposite, left, axes):
    half = own.shape[0] // 2
    low, high = shift(opposite[:half], axes, -1), shift(opposite[half:], axes, 1)
    right = jnp.concatenate([total(right[:half], low).astype(bf16), right[half:]], axis=0)
    left = jnp.concatenate([left[:half], total(left[half:], high).astype(bf16)], axis=0)
    return total(own, shift(right, axes, -1), shift(left, axes, 1)).astype(bf16)


def scatter_near(value, axes):
    return total(
        value[0], shift(value[1], axes, -1), shift(value[2], axes, 2), shift(value[3], axes, 1)
    )


def per_device(
    residual_in,
    query_latent,
    latent_cache,
    new_latent,
    context_lengths,
    value_up,
    out_proj,
    norm_gain,
    expert_ids,
    route_scores,
    expert_slots,
    expert_gate_up,
    expert_down,
):
    rows, model_width = residual_in.shape
    latent_width = value_up.shape[1]
    half = model_width // 2
    lanes = 128
    core = lax.axis_index("core")
    x_at = lax.axis_index("x")
    expert_at = lax.axis_index("y") * 4 + lax.axis_index("z")

    def mine(value, axis):
        return lax.dynamic_slice_in_dim(value, core * half, half, axis=axis)

    def others(value, axis):
        return lax.dynamic_slice_in_dim(value, (1 - core) * half, half, axis=axis)

    def by_core(own, got):
        return jnp.where(core == 0, jnp.stack([own, got]), jnp.stack([got, own]))

    def to_tokens(chip):
        own = jnp.where(core == 0, chip[0], chip[1])
        got = swap(jnp.where(core == 0, chip[1], chip[0]))
        return jnp.where(
            core == 0,
            jnp.concatenate([own, got], axis=1),
            jnp.concatenate([got, own], axis=1),
        )

    gates = (route_scale * route_scores / jnp.sum(route_scores, axis=1, keepdims=True)).astype(bf16)
    table = combine_table(expert_ids, gates, expert_slots)
    table = jnp.pad(table, ((0, 0), (0, lanes - table.shape[1])))

    latent_out = attend(query_latent, latent_cache, new_latent, context_lengths, latent_width)
    exchanged = lax.all_to_all(latent_out, ("x", "core"), split_axis=1, concat_axis=0, tiled=True)

    exchanged, expert_gate_up, expert_down = lax.optimization_barrier(
        (exchanged, expert_gate_up, expert_down)
    )
    gate_up = expert_gate_up[0]
    down = expert_down[0]
    gate_up_own = mine(gate_up, 1)
    gate_up_got = swap(others(gate_up, 1))
    weight_in = jnp.concatenate(
        [gate_up_own[0], gate_up_own[1], gate_up_got[0], gate_up_got[1]], axis=1
    )
    weight_in = jnp.pad(weight_in, ((0, lanes), (0, 0)))
    weight_out = jnp.concatenate([mine(down, 1), swap(others(down, 1))], axis=0)

    chip_rows = by_core(
        jnp.concatenate([mine(residual_in, 1), table], axis=1),
        swap(jnp.concatenate([others(residual_in, 1), table], axis=1)),
    ).reshape(2 * rows, half + lanes)
    chip_residual, chip_table = chip_rows[:, :half], chip_rows[:, half:]

    values = jnp.einsum(
        "thl,hlv->thv", exchanged, value_up, preferred_element_type=f32
    ).astype(bf16)
    values = values.reshape(values.shape[0], values.shape[1] * values.shape[2])
    projected = jnp.dot(values, out_proj, preferred_element_type=f32)
    chip_sum = mine(projected, 1) + swap(others(projected, 1).astype(bf16)).astype(f32)
    chip_sum = chip_sum.reshape(4, 2 * rows, half)

    def for_chip(distance):
        place = lax.rem(x_at + distance, 4)
        return lax.dynamic_index_in_dim(chip_sum, place, axis=0, keepdims=False)

    attention = total(
        for_chip(0),
        shift(for_chip(1).astype(bf16), ("x", "x"), -1),
        shift(for_chip(2).astype(bf16), ("x", "x"), 2),
        shift(for_chip(3).astype(bf16), ("x", "x"), 1),
    ).astype(bf16)
    residual_f32 = total(chip_residual, attention).astype(bf16).astype(f32)
    squares = jnp.sum(residual_f32 * residual_f32, axis=1, keepdims=True)
    squares = squares + swap(squares)
    scaling = lax.rsqrt(squares / model_width + norm_eps)
    gain = mine(norm_gain, 0).astype(f32)
    normed = (residual_f32 * scaling * gain[None, :]).astype(bf16)
    payload = jnp.concatenate([normed, chip_table], axis=1)

    width = half + lanes
    group = gather_near(payload, first_axis).reshape(8 * rows, width)
    near = gather_near(group, near_axis).reshape(4, 4, 2, rows, width)
    near, weight_out = lax.optimization_barrier((near, weight_out))

    chunks = [near[:, :, c].reshape(16 * rows, width) for c in range(2)]
    hidden = weight_in.shape[1] // 2
    units = hidden // 2

    def crossed(value):
        value = value.reshape(4, 4, 4, rows, value.shape[1])
        value = jnp.where(
            core == 0, value.transpose(2, 0, 1, 3, 4), value.transpose(1, 2, 0, 3, 4)
        )
        return value.reshape(64 * rows, value.shape[4])

    sums = []
    for chunk in chunks:
        blocks = gather_far(chunk, far_axis)
        products = [jnp.dot(b, weight_in, preferred_element_type=f32) for b in blocks]
        got = swap(jnp.concatenate([p[:, hidden:].astype(bf16) for p in products], axis=0))
        product = jnp.concatenate([p[:, :hidden] for p in products], axis=0)
        product = product + crossed(got).astype(f32)
        activated = (jax.nn.silu(product[:, :units]) * product[:, units:]).astype(bf16)
        activated = jnp.concatenate([activated, crossed(swap(activated))], axis=1)
        labels = lax.broadcasted_iota(jnp.int32, (1, lanes), 1)
        weights = jnp.concatenate(
            [
                jnp.sum(
                    jnp.where(labels == expert_at, b[:, half:].astype(f32), 0.0),
                    axis=1,
                    keepdims=True,
                )
                for b in blocks
            ],
            axis=0,
        )
        out = jnp.dot(activated, weight_out, preferred_element_type=f32)
        out = (out * weights).astype(bf16)
        n = 16 * rows
        outs = [out[i * n : (i + 1) * n] for i in range(4)]
        back = scatter_far(*outs, far_axis).reshape(4, 4 * rows, half)
        sums.append(scatter_near(back, near_axis).astype(bf16))
    to_x = jnp.stack([s.reshape(4, rows, half) for s in sums], axis=1)
    chip_out = scatter_near(to_x, first_axis)

    attention_out = to_tokens(attention.reshape(2, rows, half))
    expert_sum = to_tokens(chip_out.astype(bf16))
    residual_mid = total(residual_in, attention_out).astype(bf16)
    layer_output = total(residual_mid, expert_sum).astype(bf16)
    return (attention_out, layer_output)


def solution(mesh):
    torus = Mesh(mesh.devices.reshape(4, 4, 4, 2), ("y", "z", "x", "core"))
    dp, tp = ("y", "z"), ("x", "core")
    both = dp + tp
    placed = (
        P(both, None),
        P(both, None, None),
        P(both, None, None),
        P(both, None),
        P(both),
        P(tp, None, None),
        P(tp, None),
        P(),
        P(both, None),
        P(both, None),
        P(),
        P(dp, None, None, tp),
        P(dp, tp, None),
    )
    return jax.shard_map(
        per_device,
        mesh=torus,
        in_specs=placed,
        out_specs=(P(both, None), P(both, None)),
        check_vma=False,
    )
```
